256 devices in a mesh: dp: 16 (over z_lo, y), seq: 16 (over z_hi, x, core).
Axes of the slice: x: 4, y: 4, z: 8 (z_hi: 2, z_lo: 4; z = z_hi * 4 + z_lo), core: 2. Of those that a mesh axis runs over, the one named last changes fastest.
Arguments:
- layer_input: bfloat16 [16, 2048, 2048], P('dp', 'seq'), may hold values from -6 to 6
- writes_first: bfloat16 [16, 2048, 128], P('dp', 'seq'), may hold values from -0.25 to 0.25
- reads_first: bfloat16 [16, 2048, 128], P('dp', 'seq'), may hold values from -0.25 to 0.25
- decay_first: float32 [16, 32, 2048], P('dp', None, 'seq'), may hold values from -1.5 to 0, as said below
- skip_first: float32 [32], replicated, may hold values from 0.5 to 1.5
- writes_second: bfloat16 [16, 2048, 128], P('dp', 'seq'), may hold values from -0.25 to 0.25
- reads_second: bfloat16 [16, 2048, 128], P('dp', 'seq'), may hold values from -0.25 to 0.25
- decay_second: float32 [16, 32, 2048], P('dp', None, 'seq'), may hold values from -1.5 to 0, as said below
- skip_second: float32 [32], replicated, may hold values from 0.5 to 1.5
- order_first: int32 [2048], P('seq'), may hold values from 0 to 2047, as said below
- order_second: int32 [2048], P('seq'), may hold values from 0 to 2047, as said below
- cotangent: float32 [16, 2048, 2048], P('dp', 'seq'), may hold values from -48 to 48
Outputs:
- grad_input: bfloat16 [16, 2048, 2048], P('dp', 'seq')
- grad_writes_first: bfloat16 [16, 2048, 128], P('dp', 'seq')
- grad_reads_first: bfloat16 [16, 2048, 128], P('dp', 'seq')
- grad_decay_first: float32 [16, 32, 2048], P('dp', None, 'seq')
- grad_skip_first: float32 [32], replicated
- grad_writes_second: bfloat16 [16, 2048, 128], P('dp', 'seq')
- grad_reads_second: bfloat16 [16, 2048, 128], P('dp', 'seq')
- grad_decay_second: float32 [16, 32, 2048], P('dp', None, 'seq')
- grad_skip_second: float32 [32], replicated
The draws below stay inside these ranges and needn't reach their ends.
Inputs may be any that keep to these rules, and one draw needn't show every extreme that they name: order_first lists the cells of a 64 by 32 grid (cell i * 32 + j for row i, column j) row after row from row 0 on, each row left to right or right to left. order_second lists the same cells column after column from column 0 on, each column top to bottom or bottom to top. `decay_first`: every entry is negative. `decay_second`: every entry is negative.
All inputs are finite; a program needn't handle non-finite values.
Results may differ from the reference program's by a relative error of at most 0.005.
Values may be sent and summed in bfloat16 or wider, within the bound.
No kernel may reach another device: no remote copies, remote signals or barrier semaphores. Data moves between devices by JAX's collectives and lax.ppermute only.
A program may use at most 128 MiB of HBM per device.

```python
import math
import jax
import jax.numpy as jnp
from jax import lax

HEADS = 32
HEAD_DIM = 64
STATE = 128
GROUP = 128
COLS = 32
WIDTH = 2048
ROWS = 64
CLIP_TOKENS = 2048
CLIP_COUNT = 16


def decay_law(key):
    random_key_sequence = jax.random.split(key, 6)
    fast_share = 0.5
    is_fast = jax.random.uniform(random_key_sequence[0], (HEADS,)) < fast_share
    fast_rate = jnp.exp(jax.random.uniform(random_key_sequence[1], (HEADS,), minval=jnp.log(1.0 / 50.0), maxval=jnp.log(1.0 / 30.0)))
    slow_rate = jnp.exp(jax.random.uniform(random_key_sequence[2], (HEADS,), minval=jnp.log(0.05), maxval=jnp.log(0.35))) / CLIP_TOKENS
    base_rate = jnp.where(is_fast, fast_rate, slow_rate)
    roughness = jax.random.uniform(random_key_sequence[3], (CLIP_COUNT, HEADS, CLIP_TOKENS), minval=0.5, maxval=1.5)
    block_scale = jnp.exp(jax.random.uniform(random_key_sequence[4], (CLIP_COUNT, 1, CLIP_TOKENS // GROUP), minval=jnp.log(0.6), maxval=jnp.log(1.6)))
    block_scale = jnp.repeat(block_scale, GROUP, axis=2)
    decay_rate_every = base_rate[None, :, None] * roughness * block_scale
    spike_random_keys = jax.random.split(random_key_sequence[5], 2)
    spike_location = jax.random.randint(spike_random_keys[0], (CLIP_COUNT, 2), 0, CLIP_TOKENS)
    spike_penalty_loss = jax.random.uniform(spike_random_keys[1], (CLIP_COUNT, 2), minval=0.2, maxval=0.5)
    token_position = jnp.arange(CLIP_TOKENS, dtype=jnp.int32)
    spike_penalty_terms = (token_position[None, None, :] == spike_location[:, :, None]).astype(jnp.float32) * jnp.log(1.0 - spike_penalty_loss)[:, :, None]
    return (jnp.sum(spike_penalty_terms, axis=1)[:, None, :] - decay_rate_every).astype(jnp.float32)


def draw_decay_first(key, part):
    return decay_law(jax.random.fold_in(key, 11))


def draw_decay_second(key, part):
    return decay_law(jax.random.fold_in(key, 12))


def draw_order_first(key, part):
    reversed_rows = jax.random.randint(jax.random.fold_in(key, 21), (ROWS,), 0, 2)
    token_position = jnp.arange(CLIP_TOKENS, dtype=jnp.int32)
    row_ids = token_position // COLS
    col_ids = token_position % COLS
    return (row_ids * COLS + jnp.where(reversed_rows[row_ids] == 1, COLS - 1 - col_ids, col_ids)).astype(jnp.int32)


def draw_order_second(key, part):
    reversed_cols = jax.random.randint(jax.random.fold_in(key, 22), (COLS,), 0, 2)
    token_position = jnp.arange(CLIP_TOKENS, dtype=jnp.int32)
    col_ids = token_position // ROWS
    row_ids = token_position % ROWS
    return (jnp.where(reversed_cols[col_ids] == 1, ROWS - 1 - row_ids, row_ids) * COLS + col_ids).astype(jnp.int32)


def draw_cotangent(key, part):
    key_one = jax.random.fold_in(key, 31)
    clip_rise = 3.0 ** (jnp.arange(CLIP_COUNT, dtype=jnp.float32) / CLIP_COUNT)
    token_position = jnp.arange(CLIP_TOKENS, dtype=jnp.float32) / CLIP_TOKENS
    noise_all = jnp.clip(jax.random.normal(key_one, (CLIP_COUNT, CLIP_TOKENS, HEADS * HEAD_DIM)), -5.0, 5.0)
    seq_rise = 3.0 ** token_position
    return (noise_all * clip_rise[:, None, None] * seq_rise[None, :, None]).astype(jnp.float32)


def steps_of(own_key, shape, cuts, least, high):
    gain = 1.0
    for dim, shards_of in cuts:
        draws = jax.random.uniform(jax.random.fold_in(jax.random.fold_in(own_key, 6), dim), (shards_of,), jnp.float32, least / len(cuts), high / len(cuts))
        gain = gain * jnp.repeat(jnp.exp(draws), shape[dim] // shards_of).reshape((-1,) + (1,) * (len(shape) - 1 - dim))
    return gain


def noise(rng, dims, deviation, bound, shards=(), kind=jnp.bfloat16):
    drawn = jax.random.normal(rng, dims, jnp.float32) * deviation
    if len(shards) > 0:
        drawn = steps_of(rng, dims, shards, -0.22, 0.18) * drawn
    return jnp.clip(drawn, min=-bound, max=bound).astype(kind)


def setup_inputs(seed: int = 0) -> dict:
    keys = jax.random.split(jax.random.key(seed), 13)
    return {
        "layer_input": noise(keys[0], (CLIP_COUNT, CLIP_TOKENS, WIDTH), 1.0, 6.0, ((0, 16), (1, 16))),
        "writes_first": noise(keys[1], (CLIP_COUNT, CLIP_TOKENS, STATE), ((CLIP_TOKENS * STATE) ** -0.25), 0.25, ((0, 16), (1, 16))),
        "reads_first": noise(keys[2], (CLIP_COUNT, CLIP_TOKENS, STATE), ((CLIP_TOKENS * STATE) ** -0.25), 0.25, ((0, 16), (1, 16))),
        "decay_first": draw_decay_first(jax.random.fold_in(keys[12], 71), 0),
        "skip_first": jnp.clip(jax.random.uniform(keys[4], (HEADS,), jnp.float32, 0.5, 1.5), 0.5, 1.5),
        "writes_second": noise(keys[5], (CLIP_COUNT, CLIP_TOKENS, STATE), ((CLIP_TOKENS * STATE) ** -0.25), 0.25, ((0, 16), (1, 16))),
        "reads_second": noise(keys[6], (CLIP_COUNT, CLIP_TOKENS, STATE), ((CLIP_TOKENS * STATE) ** -0.25), 0.25, ((0, 16), (1, 16))),
        "decay_second": draw_decay_second(jax.random.fold_in(keys[12], 71), 0),
        "skip_second": jnp.clip(jax.random.uniform(keys[8], (HEADS,), jnp.float32, 0.5, 1.5), 0.5, 1.5),
        "order_first": draw_order_first(jax.random.fold_in(keys[12], 71), 0),
        "order_second": draw_order_second(jax.random.fold_in(keys[12], 71), 0),
        "cotangent": draw_cotangent(jax.random.fold_in(keys[12], 71), 0),
    }


highest = lax.Precision.HIGHEST

def group_step(carried, pieces, skip):
    inputs, writes, reads, log_decay = pieces
    running = jnp.cumsum(log_decay, axis=0)
    length = inputs.shape[0]
    causal = jnp.tril(jnp.ones((length, length), dtype=bool))
    scores = jnp.dot(reads, writes.T, precision=highest)
    log_gap = running.T[:, :, None] - running.T[:, None, :]
    weights = jnp.where(causal[None], jnp.exp(jnp.where(causal[None], log_gap, 0.0)), 0.0) * scores[None]
    outputs = jnp.einsum('hts,shp->thp', weights, inputs, precision=highest)
    carried_out = jnp.einsum('hpn,tn->thp', carried, reads, precision=highest)
    outputs = outputs + jnp.exp(running)[:, :, None] * carried_out + skip[None, :, None] * inputs
    totals = running[-1]
    scaled = inputs * jnp.exp(totals[None, :] - running)[:, :, None]
    carried = jnp.exp(totals)[:, None, None] * carried + jnp.einsum('shp,sn->hpn', scaled, writes, precision=highest)
    return (carried, outputs)

def run_layer(inputs, writes, reads, log_decay, skip, carried):
    length, features = inputs.shape
    head_count = log_decay.shape[1]
    head_size = features // head_count
    block_count = length // GROUP
    stacked = (inputs.reshape(block_count, GROUP, head_count, head_size), writes.reshape(block_count, GROUP, writes.shape[1]), reads.reshape(block_count, GROUP, reads.shape[1]), log_decay.reshape(block_count, GROUP, head_count))
    carried, outputs = lax.scan(lambda carry_now, pieces: group_step(carry_now, pieces, skip), carried, stacked)
    return (outputs.reshape(length, features), carried)

def reference(layer_input, writes_first, reads_first, decay_first, skip_first, writes_second, reads_second, decay_second, skip_second, order_first, order_second, cotangent):
    features = HEADS * HEAD_DIM
    empty_state = jnp.zeros((HEADS, HEAD_DIM, STATE), jnp.float32)

    def layer_pair(inputs, writes_one, reads_one, decay_one, skip_one, writes_two, reads_two, decay_two, skip_two):
        first_out = run_layer(inputs.astype(jnp.float32), writes_one.astype(jnp.float32), reads_one.astype(jnp.float32), decay_one.T, skip_one, empty_state)[0]
        lattice = jnp.zeros((CLIP_TOKENS, features), jnp.bfloat16).at[order_first].set(first_out.astype(jnp.bfloat16))
        second_in = lattice[order_second]
        return run_layer(second_in.astype(jnp.float32), writes_two.astype(jnp.float32), reads_two.astype(jnp.float32), decay_two.T, skip_two, empty_state)[0]

    def per_clip(pieces):
        inputs, writes_one, reads_one, decay_one, writes_two, reads_two, decay_two, upstream = pieces
        _, pullback = jax.vjp(layer_pair, inputs, writes_one, reads_one, decay_one, skip_first, writes_two, reads_two, decay_two, skip_second)
        return pullback(upstream)
    grads = lax.map(per_clip, (layer_input, writes_first, reads_first, decay_first, writes_second, reads_second, decay_second, cotangent))
    factor = 1.0 / math.sqrt(CLIP_COUNT * CLIP_TOKENS * HEAD_DIM)
    return (grads[0], grads[1], grads[2], grads[3], lax.optimization_barrier(jnp.sum(grads[4], axis=0)) * factor, grads[5], grads[6], grads[7], lax.optimization_barrier(jnp.sum(grads[8], axis=0)) * factor)
```

```python
import functools
import math

import jax
import jax.numpy as jnp
from jax import lax
from jax.experimental import pallas as pl
from jax.experimental.pallas import tpu as pltpu
from jax.sharding import Mesh
from jax.sharding import PartitionSpec as P

COLS = 32
ROWS = 64
BLOCK = 128
HALF = 64
LANES = 128
PART_ROWS = 784
SHARED_ROWS = 528
SEND_ROWS = 2 * PART_ROWS + SHARED_ROWS
OUT_ROWS = 784
BACK_ROWS = 1088

f32 = jnp.float32
bf16 = jnp.bfloat16


def nn(a, b):
    return lax.dot_general(a, b, (((1,), (0,)), ((), ())), preferred_element_type=f32)


def nt(a, b):
    return lax.dot_general(a, b, (((1,), (1,)), ((), ())), preferred_element_type=f32)


def tn(a, b):
    return lax.dot_general(a, b, (((0,), (0,)), ((), ())), preferred_element_type=f32)


def down(*values):
    return jnp.concatenate(values, axis=0)


def across(*values):
    return jnp.concatenate(values, axis=1)


def parts(values):
    hi = values.astype(bf16)
    return hi, (values - hi.astype(f32)).astype(bf16)


def iota(dim):
    return lax.broadcasted_iota(jnp.int32, (BLOCK, BLOCK), dim)


def one_where(cond):
    return jnp.where(cond, f32(1.0), f32(0.0))


def constants():
    row, col = iota(0), iota(1)
    lower = one_where(col <= row)
    before = one_where(row < col)
    after = one_where(row > col).astype(bf16)
    head_a = one_where(col < HALF)
    head_b = 1.0 - head_a
    wide_a, wide_b = across(after, head_a.astype(bf16)), across(after, head_b.astype(bf16))
    head_a, head_b = head_a.astype(bf16), head_b.astype(bf16)
    return {
        "lower": lower,
        "head_a": head_a,
        "head_b": head_b,
        "heads": down(head_a, head_a, head_b, head_b),
        "spread_a": down(wide_a, wide_a),
        "spread_b": down(wide_b, wide_b),
        "lower_bf": lower.astype(bf16),
        "before": before,
        "sums": down(lower, before, jnp.ones((BLOCK, BLOCK), f32)).astype(bf16),
        "same": one_where(row == col),
        "mirror_row": one_where(row + col == 2 * (row - row % COLS) + COLS - 1),
        "mirror_col": one_where(row + col == 2 * (row - row % ROWS) + ROWS - 1),
    }


def masked_decays(c, tok_ref, b, layer, group):
    small = tok_ref[b, 768:784, :].astype(f32)
    at = 4 * layer + 2 * group

    def one(k):
        return across(
            (c["lower"] * small[at + k : at + k + 1]).astype(bf16),
            (c["lower"] * small[8 + at + k : 9 + at + k]).astype(bf16),
        )

    return one(0), one(1)


def scales(running):
    total = running[BLOCK - 1 : BLOCK, :]
    return jnp.exp(running), jnp.exp(total - running), jnp.exp(total)


def decay_scales(c, tok_ref, b, layer, group):
    a, h = masked_decays(c, tok_ref, b, layer, group)
    return scales(nn(across(a, h), c["heads"]))


def decay_block(c, tok_ref, b, layer, group):
    a, h = masked_decays(c, tok_ref, b, layer, group)
    a, h = nn(a, c["spread_a"]), nn(h, c["spread_b"])
    decay_a = jnp.exp(a[:, :BLOCK]) * c["lower"]
    decay_b = jnp.exp(h[:, :BLOCK]) * c["lower"]
    return (decay_a, decay_b, *scales(a[:, BLOCK:] + h[:, BLOCK:]))


def by_head(c, values):
    return down(values * c["head_a"], values * c["head_b"])


def mirror(c, sh_ref, b, layer):
    flags = sh_ref[b, 512:528, :].astype(f32)[layer : layer + 1]
    turned = c["mirror_col"] if layer else c["mirror_row"]
    return (flags * turned + (1.0 - flags) * c["same"]).astype(bf16)


def vectors(sh_ref, b, layer):
    at = 256 * layer
    return sh_ref[b, at : at + 128, :], sh_ref[b, at + 128 : at + 256, :]


def inputs_of(tok_ref, b, group):
    return tok_ref[b, 128 * group : 128 * group + 128, :]


def cotangent_of(tok_ref, b, group):
    at = 256 + 128 * group
    return tok_ref[b, at : at + 128, :], tok_ref[b, at + 256 : at + 384, :]


def pack_kernel(u_ref, cot_ref, decay_ref, w1, r1, w2, r2, flags_ref, out_ref):
    for dest in range(8):
        x, core = dest // 2, dest % 2
        at = core * PART_ROWS
        for group in range(2):
            lanes = slice((2 * dest + group) * LANES, (2 * dest + group + 1) * LANES)
            row = at + 128 * group
            out_ref[x, row : row + 128, :] = u_ref[:, lanes]
            hi, lo = parts(cot_ref[:, lanes])
            out_ref[x, row + 256 : row + 384, :] = hi
            out_ref[x, row + 512 : row + 640, :] = lo
        decays = down(*(decay_ref[layer, 4 * dest : 4 * dest + 4, :] for layer in range(2)))
        hi, lo = parts(decays)
        out_ref[x, at + 768 : at + 784, :] = down(hi.astype(f32), lo.astype(f32)).astype(bf16)
    for x in range(4):
        at = 2 * PART_ROWS
        for k, ref in enumerate((w1, r1, w2, r2)):
            out_ref[x, at + 128 * k : at + 128 * (k + 1), :] = ref[...]
        out_ref[x, at + 512 : at + 528, :] = flags_ref[...]


def update(c, scale, carry, vector, values):
    return scale * carry + tn(down(vector, vector), down(*parts(values)))


def gather_kernel(place_ref, own_ref, other_ref, tok_ref, sh_ref, ends_ref, s_ref, a_ref):
    z, core = place_ref[0], place_ref[2]
    for x in range(4):
        start = pl.multiple_of(core * PART_ROWS, 16)
        tok_ref[2 * x + core] = own_ref[x, pl.ds(start, PART_ROWS), :]
        tok_ref[2 * x + 1 - core] = other_ref[x, 0:PART_ROWS, :]
        sh_ref[2 * x + core] = own_ref[x, 2 * PART_ROWS :, :]
        sh_ref[2 * x + 1 - core] = other_ref[x, PART_ROWS:, :]
    c = constants()
    s_ref[...] = jnp.zeros_like(s_ref)
    a_ref[...] = jnp.zeros_like(a_ref)

    def step(i, _):
        b = i
        writes, _reads = vectors(sh_ref, b, 0)
        for group in range(2):
            _grown, left, total = decay_scales(c, tok_ref, b, 0, group)
            u = inputs_of(tok_ref, b, group).astype(f32)
            s_ref[group] = update(c, total, s_ref[group], writes, u * left)
        b = 7 - i
        _writes, reads = vectors(sh_ref, b, 1)
        for group in range(2):
            grown, _left, total = decay_scales(c, tok_ref, b, 1, group)
            hi, lo = cotangent_of(tok_ref, b, group)
            dy = hi.astype(f32) + lo.astype(f32)
            a_ref[group] = update(c, total, a_ref[group], reads, dy * grown)
        return 0

    lax.fori_loop(0, 8, step, 0)
    ends_ref[...] = jnp.where(z == 0, s_ref[...], a_ref[...])


def first_kernel(
    place_ref, tok_ref, sh_ref, skip_ref, ends_ref, keep_ref, send_ref, state_ref, adjoint_ref, s_ref, a_ref
):
    z = place_ref[0]
    c = constants()
    s_ref[...] = jnp.where(z == 1, ends_ref[...], 0.0)
    a_ref[...] = jnp.where(z == 0, ends_ref[...], 0.0)

    def step(i, _):
        b = i
        writes, reads = vectors(sh_ref, b, 0)
        scores = nt(reads, writes)
        turn = mirror(c, sh_ref, b, 0)
        for group in range(2):
            decay_a, decay_b, grown, left, total = decay_block(c, tok_ref, b, 0, group)
            u = inputs_of(tok_ref, b, group)
            mixed = across(*parts(across(decay_a * scores, decay_b * scores)))
            state = s_ref[group]
            state_both = down(*parts(state))
            state_ref[b, group] = state_both
            u32 = u.astype(f32)
            heads = by_head(c, u)
            y = (
                nn(mixed, down(heads, heads))
                + grown * nn(across(reads, reads), state_both)
                + skip_ref[group : group + 1, :] * u32
            )
            s_ref[group] = update(c, total, state, writes, u32 * left)
            grid = nn(turn, y.astype(bf16)).astype(bf16)
            for k in range(4):
                near, far = grid[32 * k : 32 * k + 16], grid[32 * k + 16 : 32 * k + 32]
                at = pl.multiple_of(64 * b + 16 * k, 16)
                keep_ref[0, group, pl.ds(at, 16), :] = jnp.where(z == 0, near, far)
                send_ref[0, group, pl.ds(at, 16), :] = jnp.where(z == 0, far, near)

        b = 7 - i
        writes, reads = vectors(sh_ref, b, 1)
        scores = nt(reads, writes)
        turn = mirror(c, sh_ref, b, 1)
        for group in range(2):
            decay_a, decay_b, grown, left, total = decay_block(c, tok_ref, b, 1, group)
            hi, lo = cotangent_of(tok_ref, b, group)
            mixed, mixed_low = parts(down(decay_a * scores, decay_b * scores))
            adjoint = a_ref[group]
            adjoint_both = down(*parts(adjoint))
            adjoint_ref[b, group] = adjoint_both
            dy = hi.astype(f32) + lo.astype(f32)
            hi_heads, lo_heads = by_head(c, hi), by_head(c, lo)
            du = (
                tn(down(mixed, mixed_low, mixed), down(hi_heads, hi_heads, lo_heads))
                + left * nn(across(writes, writes), adjoint_both)
                + skip_ref[2 + group : 3 + group, :] * dy
            )
            a_ref[group] = update(c, total, adjoint, reads, dy * grown)
            grid = nn(turn, du.astype(bf16)).astype(bf16)
            for k in range(2):
                near, far = grid[64 * k : 64 * k + 32], grid[64 * k + 32 : 64 * k + 64]
                at = pl.multiple_of(64 * b + 32 * k, 32)
                keep_ref[1, group, pl.ds(at, 32), :] = jnp.where(z == 0, near, far)
                send_ref[1, group, pl.ds(at, 32), :] = jnp.where(z == 0, far, near)
        return 0

    lax.fori_loop(0, 8, step, 0)


def regrid_kernel(
    place_ref, tok_ref, sh_ref, keep_ref, got_ref, u2_ref, dy1_ref, ends_ref, skip_ref, grid_ref, s_ref, a_ref
):
    z = place_ref[0]
    c = constants()
    grid_ref[z] = keep_ref[...].astype(f32)
    grid_ref[1 - z] = got_ref[...].astype(f32)
    s_ref[...] = jnp.zeros_like(s_ref)
    a_ref[...] = jnp.zeros_like(a_ref)
    skip_ref[...] = jnp.zeros_like(skip_ref)

    def step(i, _):
        b = i
        writes, _reads = vectors(sh_ref, b, 1)
        turn = mirror(c, sh_ref, b, 1)
        for group in range(2):
            picked = down(
                *(
                    grid_ref[part, 0, group, pl.ds(2 * b + k, 32, stride=16), :]
                    for k in range(2)
                    for part in range(2)
                )
            )
            u32 = nn(turn, picked.astype(bf16))
            u2_ref[b, group] = u32.astype(bf16)
            _grown, left, total = decay_scales(c, tok_ref, b, 1, group)
            s_ref[group] = update(c, total, s_ref[group], writes, u32 * left)
            hi, lo = cotangent_of(tok_ref, b, group)
            dy = hi.astype(f32) + lo.astype(f32)
            skip_ref[2 + group : 3 + group, :] += jnp.sum(u32 * dy, axis=0, keepdims=True)
        b = 7 - i
        _writes, reads = vectors(sh_ref, b, 0)
        turn = mirror(c, sh_ref, b, 0)
        for group in range(2):
            picked = down(
                *(
                    grid_ref[part, 1, group, pl.ds(4 * b + k, 16, stride=32), :]
                    for k in range(4)
                    for part in range(2)
                )
            )
            dy = nn(turn, picked.astype(bf16))
            dy1_ref[b, group] = dy.astype(bf16)
            grown, _left, total = decay_scales(c, tok_ref, b, 0, group)
            a_ref[group] = update(c, total, a_ref[group], reads, dy * grown)
            u = inputs_of(tok_ref, b, group).astype(f32)
            skip_ref[group : group + 1, :] += jnp.sum(u * dy, axis=0, keepdims=True)
        return 0

    lax.fori_loop(0, 8, step, 0)
    ends_ref[...] = jnp.where(z == 0, s_ref[...], a_ref[...])


def block_gradients(c, tok_ref, sh_ref, b, layer, u_of, dy_of, state_of, adjoint_of):
    writes, reads = vectors(sh_ref, b, layer)
    reads_two, writes_two = down(reads, reads), down(writes, writes)
    scores = nt(reads, writes)
    d_scores, d_writes, d_reads = 0.0, 0.0, 0.0
    decay_rows, kept = [], []
    for group in range(2):
        decay_a, decay_b, grown, left, total = decay_block(c, tok_ref, b, layer, group)
        u, (dy, dy_low) = u_of(group), dy_of(group)
        u32, dy32 = u.astype(f32), dy.astype(f32)
        dy_heads = by_head(c, dy)
        if dy_low is None:
            pairs = nt(dy_heads, u)
        else:
            pairs = nt(across(dy_heads, by_head(c, dy_low)), across(u, u))
            dy32 = dy32 + dy_low.astype(f32)
        pair_a, pair_b = decay_a * pairs[:BLOCK], decay_b * pairs[BLOCK:]
        d_scores = d_scores + pair_a + pair_b
        u_left, dy_grown = u32 * left, dy32 * grown
        u_hi, u_lo = parts(u_left)
        dy_hi, dy_lo = parts(dy_grown)
        state, adjoint = state_of(group), adjoint_of(group)
        read_state = nn(across(reads, reads), state)
        write_adjoint = nn(across(writes, writes), adjoint)
        state_hi, adjoint_hi = state[:LANES], adjoint[:LANES]
        d_writes = (
            d_writes
            + nt(across(u_hi, u_lo), across(adjoint_hi, adjoint_hi))
            + nt(u_hi, adjoint[LANES:])
        )
        d_reads = (
            d_reads
            + nt(across(dy_hi, dy_lo), across(state_hi, state_hi))
            + nt(dy_hi, state[LANES:])
        )
        crossing = across((pair_a * scores).astype(bf16), (pair_b * scores).astype(bf16))
        inner = tn(crossing, c["lower_bf"])
        products = down(
            (dy_grown * read_state).astype(bf16),
            (u_left * write_adjoint).astype(bf16),
            (total * (state_hi.astype(f32) * adjoint_hi.astype(f32))).astype(bf16),
        )
        outer = tn(products, c["sums"])
        for k in range(2):
            decay_rows.append(
                jnp.sum(c["before"] * inner[BLOCK * k : BLOCK * (k + 1)], axis=0, keepdims=True)
                + jnp.sum(outer[HALF * k : HALF * (k + 1)], axis=0, keepdims=True)
            )
        kept.append(
            {
                "total": total,
                "left": left,
                "u_left": down(u_hi, u_lo),
                "dy_grown": down(dy_hi, dy_lo),
                "write_adjoint": write_adjoint,
                "dy_heads": dy_heads,
                "dy": dy32,
                "mixed": lambda a=decay_a, h=decay_b: down(
                    (a * scores).astype(bf16), (h * scores).astype(bf16)
                ),
            }
        )
    low = parts(d_scores)
    d_writes = d_writes + tn(down(*low), reads_two)
    d_reads = d_reads + nn(across(*low), writes_two)
    return d_writes, d_reads, down(*decay_rows), kept, writes_two, reads_two


def second_kernel(
    place_ref,
    tok_ref,
    sh_ref,
    skip_ref,
    u2_ref,
    dy1_ref,
    state_ref,
    adjoint_ref,
    ends_ref,
    out_ref,
    s_ref,
    a_ref,
):
    z, core = place_ref[0], place_ref[2]
    c = constants()
    s_ref[...] = jnp.where(z == 1, ends_ref[...], 0.0)
    a_ref[...] = jnp.where(z == 0, ends_ref[...], 0.0)

    def put(b, layer, d_writes, d_reads, decay_rows):
        slot, x = jnp.bitwise_xor(b % 2, core), b // 2
        at = 256 + 256 * layer
        out_ref[slot, x, at : at + 128, :] = d_writes.astype(bf16)
        out_ref[slot, x, at + 128 : at + 256, :] = d_reads.astype(bf16)
        return decay_rows

    def step(i, _):
        b = i
        d_writes, d_reads, rows, kept, writes_two, _ = block_gradients(
            c,
            tok_ref,
            sh_ref,
            b,
            1,
            lambda g: u2_ref[b, g],
            lambda g: cotangent_of(tok_ref, b, g),
            lambda g: down(*parts(s_ref[g])),
            lambda g: adjoint_ref[b, g],
        )
        put(b, 1, d_writes, d_reads, rows)
        decay_ref_rows(out_ref, b, core, 1, rows)
        for group in range(2):
            k = kept[group]
            s_ref[group] = k["total"] * s_ref[group] + tn(writes_two, k["u_left"])
        r = 7 - i
        d_writes, d_reads, rows, kept, _, reads_two = block_gradients(
            c,
            tok_ref,
            sh_ref,
            r,
            0,
            lambda g: inputs_of(tok_ref, r, g),
            lambda g: (dy1_ref[r, g], None),
            lambda g: state_ref[r, g],
            lambda g: down(*parts(a_ref[g])),
        )
        put(r, 0, d_writes, d_reads, rows)
        decay_ref_rows(out_ref, r, core, 0, rows)
        for group in range(2):
            k = kept[group]
            du = (
                tn(k["mixed"](), k["dy_heads"])
                + k["left"] * k["write_adjoint"]
                + skip_ref[group : group + 1, :] * k["dy"]
            )
            slot = jnp.bitwise_xor(r % 2, core)
            out_ref[slot, r // 2, 128 * group : 128 * group + 128, :] = du.astype(bf16)
            a_ref[group] = k["total"] * a_ref[group] + tn(reads_two, k["dy_grown"])
        return 0

    lax.fori_loop(0, 8, step, 0)


def decay_ref_rows(out_ref, b, core, layer, rows):
    hi, lo = parts(rows)
    slot = jnp.bitwise_xor(b % 2, core)
    at = 768 + 8 * layer
    both = down(hi.astype(f32), lo.astype(f32)).astype(bf16)
    out_ref[slot, b // 2, at : at + 8, :] = both


def pair_kernel(own_ref, other_ref, skip_ref, skip_other_ref, out_ref):
    pieces = []
    for ref in (skip_ref, skip_other_ref):
        total = ref[0:4, :]
        hi, rest = parts(total)
        rest = total - hi.astype(f32)
        mid, low = parts(rest)
        pieces.append(down(hi.astype(f32), mid.astype(f32), low.astype(f32), jnp.zeros((4, LANES), f32)))
    skips = down(*pieces).astype(bf16)
    for x in range(4):
        out_ref[x, 0:256, :] = own_ref[x, 0:256, :]
        out_ref[x, 256:512, :] = other_ref[x, 0:256, :]
        out_ref[x, 512:1024, :] = (
            own_ref[x, 256:768, :].astype(f32) + other_ref[x, 256:768, :].astype(f32)
        ).astype(bf16)
        out_ref[x, 1024:1040, :] = own_ref[x, 768:784, :]
        out_ref[x, 1040:1056, :] = other_ref[x, 768:784, :]
        out_ref[x, 1056:1088, :] = skips


def last_kernel(place_ref, back_ref, grad_ref, w1, r1, w2, r2, decay1_ref, decay2_ref, skip_ref):
    core = place_ref[2]
    for x in range(4):
        for owner in range(2):
            for group in range(2):
                near = back_ref[x, 128 * group : 128 * group + 128, :]
                far = back_ref[x, 256 + 128 * group : 384 + 128 * group, :]
                at = ((2 * x + owner) * 2 + group) * LANES
                grad_ref[:, at : at + LANES] = jnp.where(core == owner, near, far)
            near = back_ref[x, 1024:1040, :].astype(f32)
            far = back_ref[x, 1040:1056, :].astype(f32)
            small = jnp.where(core == owner, near, far)
            at = (2 * x + owner) * 4
            decay1_ref[at : at + 4, :] = small[0:4] + small[4:8]
            decay2_ref[at : at + 4, :] = small[8:12] + small[12:16]
            near = back_ref[x, 1056:1072, :].astype(f32)
            far = back_ref[x, 1072:1088, :].astype(f32)
            small = jnp.where(core == owner, near, far)
            skip_ref[at : at + 4, :] = small[0:4] + small[4:8] + small[8:12]
    for k, ref in enumerate((w1, r1, w2, r2)):
        rows = slice(512 + 128 * k, 640 + 128 * k)
        total = back_ref[0, rows, :].astype(f32)
        for x in range(1, 4):
            total = total + back_ref[x, rows, :].astype(f32)
        ref[...] = total.astype(bf16)


def call(kernel, outs, scratch, *args, scalars=1):
    shapes = [jax.ShapeDtypeStruct(s, d) for s, d in outs]
    many = len(shapes) > 1
    in_specs = [pl.BlockSpec(memory_space=pltpu.SMEM)] * scalars
    in_specs += [pl.BlockSpec(memory_space=pltpu.VMEM)] * (len(args) - scalars)
    return pl.pallas_call(
        kernel,
        out_shape=shapes if many else shapes[0],
        in_specs=in_specs,
        out_specs=[pl.BlockSpec(memory_space=pltpu.VMEM)] * len(shapes)
        if many
        else pl.BlockSpec(memory_space=pltpu.VMEM),
        scratch_shapes=[pltpu.VMEM(s, d) for s, d in scratch],
        compiler_params=pltpu.CompilerParams(vmem_limit_bytes=40 * 2**20),
        name=kernel.__name__,
    )(*args)


def swap(values, axis):
    return lax.ppermute(values, axis, [(0, 1), (1, 0)])


def on_device(
    layer_input,
    writes_first,
    reads_first,
    decay_first,
    skip_first,
    writes_second,
    reads_second,
    decay_second,
    skip_second,
    order_first,
    order_second,
    cotangent,
):
    length, features = layer_input.shape[1:]
    head_count = skip_first.shape[0]
    head_size = features // head_count
    z, x, core = (lax.axis_index(a) for a in ("z", "x", "core"))
    place = jnp.stack([z, x, core]).astype(jnp.int32)

    row_flip = order_first.reshape(-1, COLS)[:, :1] % COLS != 0
    col_flip = order_second.reshape(-1, ROWS)[:, :1] // COLS != 0
    flags = jnp.concatenate(
        [
            jnp.broadcast_to(row_flip, (length // COLS, COLS)).reshape(1, length),
            jnp.broadcast_to(col_flip, (length // ROWS, ROWS)).reshape(1, length),
            jnp.zeros((14, length), bool),
        ]
    ).astype(bf16)
    packed = call(
        pack_kernel,
        [((4, SEND_ROWS, LANES), bf16)],
        [],
        layer_input[0],
        cotangent[0],
        jnp.stack([decay_first[0], decay_second[0]]),
        writes_first[0],
        reads_first[0],
        writes_second[0],
        reads_second[0],
        flags,
        scalars=0,
    )
    own = lax.all_to_all(packed, "x", split_axis=0, concat_axis=0, tiled=True)
    theirs = lax.dynamic_slice_in_dim(own, (1 - core) * PART_ROWS, PART_ROWS, axis=1)
    other = swap(jnp.concatenate([theirs, own[:, 2 * PART_ROWS :]], axis=1), "core")

    skips = jnp.stack([skip_first, skip_second])
    skips = lax.dynamic_slice_in_dim(skips, 4 * (2 * x + core), 4, axis=1)
    skips = jnp.repeat(skips, head_size, axis=1).reshape(4, LANES)
    skips = jnp.concatenate([skips, jnp.zeros((4, LANES), f32)], axis=0)

    carry = ((2, LANES, LANES), f32)
    saved = ((8, 2, 2 * LANES, LANES), bf16)
    half_grid = ((2, 2, 512, LANES), bf16)
    tok, sh, ends = call(
        gather_kernel,
        [((8, PART_ROWS, LANES), bf16), ((8, SHARED_ROWS, LANES), bf16), carry],
        [carry, carry],
        place,
        own,
        other,
    )
    ends = swap(ends, "z")
    keep, send, states, adjoints = call(
        first_kernel, [half_grid, half_grid, saved, saved], [carry, carry], place, tok, sh, skips, ends
    )
    got = swap(send, "z")
    block = ((8, 2, BLOCK, LANES), bf16)
    u2, dy1, ends, skip_sums = call(
        regrid_kernel,
        [block, block, carry, ((8, LANES), f32)],
        [((2, 2, 2, 512, LANES), f32), carry, carry],
        place,
        tok,
        sh,
        keep,
        got,
    )
    ends = swap(ends, "z")
    others = lax.axis_size("dp") * lax.axis_size("z")
    skip_sums = jnp.broadcast_to(skip_sums[None], (others, 8, LANES))
    skip_sums = lax.all_to_all(skip_sums, ("dp", "z"), split_axis=0, concat_axis=0, tiled=True)
    skip_sums = skip_sums.sum(0)
    skip_other = swap(skip_sums, "core")
    out = call(
        second_kernel,
        [((2, 4, OUT_ROWS, LANES), bf16)],
        [carry, carry],
        place,
        tok,
        sh,
        skips,
        u2,
        dy1,
        states,
        adjoints,
        ends,
    )
    from_other = swap(out[1], "core")
    back = call(
        pair_kernel,
        [((4, BACK_ROWS, LANES), bf16)],
        [],
        out[0],
        from_other,
        skip_sums,
        skip_other,
        scalars=0,
    )
    back = lax.all_to_all(back, "x", split_axis=0, concat_axis=0, tiled=True)
    vector = ((length, LANES), bf16)
    decay = ((head_count, length), f32)
    grad_input, w1, r1, w2, r2, decay1, decay2, skip_lanes = call(
        last_kernel,
        [((length, features), bf16), vector, vector, vector, vector, decay, decay, ((head_count, LANES), f32)],
        [],
        place,
        back,
    )
    seq_count = lax.axis_size("z") * lax.axis_size("x") * lax.axis_size("core")
    factor = 1.0 / math.sqrt(lax.axis_size("dp") * seq_count * length * head_size)
    skip_grads = skip_lanes.reshape(8, 2, 2, 2, head_size).sum(-1)
    skip_grads = skip_grads.transpose(1, 0, 2, 3).reshape(2, head_count) * factor
    return (
        grad_input[None],
        w1[None],
        r1[None],
        decay1[None],
        skip_grads[0],
        w2[None],
        r2[None],
        decay2[None],
        skip_grads[1],
    )


def solution(mesh):
    clips = mesh.devices.shape[0]
    finer = Mesh(mesh.devices.reshape(clips, 2, 4, 2), ("dp", "z", "x", "core"))
    seq = ("z", "x", "core")
    by_token, by_decay = P("dp", seq, None), P("dp", None, seq)
    return jax.shard_map(
        on_device,
        mesh=finer,
        in_specs=(
            by_token,
            by_token,
            by_token,
            by_decay,
            P(),
            by_token,
            by_token,
            by_decay,
            P(),
            P(seq),
            P(seq),
            by_token,
        ),
        out_specs=(
            by_token,
            by_token,
            by_token,
            by_decay,
            P(),
            by_token,
            by_token,
            by_decay,
            P(),
        ),
        check_vma=False,
    )
```

```python
import math

import jax
import jax.numpy as jnp
from jax import lax
from jax.experimental import pallas as pl
from jax.experimental.pallas import tpu as pltpu
from jax.sharding import Mesh
from jax.sharding import PartitionSpec as P

COLS = 32
ROWS = 64
BLOCK = 128
HALF = 64
LANES = 128
PART_ROWS = 784
TOKEN_ROWS = 272
SHARED_ROWS = 528
SEND_ROWS = 2 * PART_ROWS + SHARED_ROWS
COT_ROWS = 512
BLOCKS = 8
UNROLL = {"gather": 8, "first": 4, "regrid": 8, "second": 4}

f32 = jnp.float32
bf16 = jnp.bfloat16


def nn(a, b):
    return lax.dot_general(a, b, (((1,), (0,)), ((), ())), preferred_element_type=f32)


def nt(a, b):
    return lax.dot_general(a, b, (((1,), (1,)), ((), ())), preferred_element_type=f32)


def tn(a, b):
    return lax.dot_general(a, b, (((0,), (0,)), ((), ())), preferred_element_type=f32)


def down(*values):
    return jnp.concatenate(values, axis=0)


def across(*values):
    return jnp.concatenate(values, axis=1)


def parts(values):
    hi = values.astype(bf16)
    return hi, (values - hi.astype(f32)).astype(bf16)


def iota(dim):
    return lax.broadcasted_iota(jnp.int32, (BLOCK, BLOCK), dim)


def one_where(cond):
    return jnp.where(cond, f32(1.0), f32(0.0))


def constants():
    row, col = iota(0), iota(1)
    lower = one_where(col <= row)
    before = one_where(row < col)
    head_a = one_where(col < HALF)
    head_b = 1.0 - head_a
    return {
        "head_a": head_a.astype(bf16),
        "head_b": head_b.astype(bf16),
        "causal": col <= row,
        "lower_bf": lower.astype(bf16),
        "grown": spread_matrix(12, 4, 2, HALF),
        "left": spread_matrix(20, 4, 2, HALF),
        "all": across(
            spread_matrix(0, 4, 3, LANES), spread_matrix(12, 4, 2, HALF), spread_matrix(20, 4, 2, HALF)
        ),
        "before": before,
        "sums": down(lower, before, jnp.ones((BLOCK, BLOCK), f32)).astype(bf16),
        "same": one_where(row == col),
        "mirror_row": one_where(row + col == 2 * (row - row % COLS) + COLS - 1),
        "mirror_col": one_where(row + col == 2 * (row - row % ROWS) + ROWS - 1),
    }


def decay_rows_of(tok_ref):
    small = down(*(tok_ref[b, 256:272, :] for b in range(BLOCKS)))
    row, col = iota(0), iota(1)
    sums = nn(small, one_where(row <= col).astype(bf16)).reshape(BLOCKS, 16, LANES)
    running = sums[:, 0:8] + sums[:, 8:16]
    hi = running.astype(bf16).astype(f32)
    mid = (running - hi).astype(bf16).astype(f32)
    grown = jnp.exp(running)
    left = jnp.exp(running[:, :, LANES - 1 :] - running)
    grown_hi, left_hi = grown.astype(bf16).astype(f32), left.astype(bf16).astype(f32)
    pieces = (hi, mid, running - hi - mid, grown_hi, grown - grown_hi, left_hi, left - left_hi)
    zeros = jnp.zeros((BLOCKS, 4, LANES), f32)
    layers = [
        jnp.concatenate([p[:, 4 * k : 4 * k + 4] for p in pieces] + [zeros], axis=1) for k in range(2)
    ]
    return running, [one.astype(bf16) for one in layers]


def spread_matrix(first, count, copies, width):
    row = lax.broadcasted_iota(jnp.int32, (32, count * width), 0)
    col = lax.broadcasted_iota(jnp.int32, (32, count * width), 1)
    inside = (row >= first) & (row < first + copies * count)
    return one_where(inside & ((row - first) % count == col // width)).astype(bf16)


def decay_scales(c, rows_ref, b, layer, which):
    rows = rows_ref[layer, b]
    values = tn(rows, c[which])
    if which == "grown":
        total = values[BLOCK - 1 :, :]
    else:
        total = tn(rows, c["grown"])[BLOCK - 1 :, :]
    return [(values[:, LANES * g : LANES * g + LANES], total[:, LANES * g : LANES * g + LANES]) for g in range(2)]


def decay_block(c, rows_ref, run_ref, b, layer):
    rows = rows_ref[layer, b]
    values = tn(rows, c["all"])
    running = run_ref[b]
    decays = [
        jnp.where(
            c["causal"],
            jnp.exp(
                jnp.minimum(
                    values[:, LANES * k : LANES * k + LANES] - running[4 * layer + k : 4 * layer + k + 1], 0.0
                )
            ),
            0.0,
        )
        for k in range(4)
    ]
    both = []
    for g in range(2):
        grown = values[:, 512 + LANES * g : 640 + LANES * g]
        left = values[:, 768 + LANES * g : 896 + LANES * g]
        both.append((decays[2 * g], decays[2 * g + 1], grown, left, grown[BLOCK - 1 :, :]))
    return both


def by_head(c, values):
    return down(values * c["head_a"], values * c["head_b"])


def mirror(c, sh_ref, b, layer):
    flags = sh_ref[b, 512:528, :].astype(f32)[layer : layer + 1]
    turned = c["mirror_col"] if layer else c["mirror_row"]
    return (flags * turned + (1.0 - flags) * c["same"]).astype(bf16)


def vectors(sh_ref, b, layer):
    at = 256 * layer
    return sh_ref[b, at : at + 128, :], sh_ref[b, at + 128 : at + 256, :]


def inputs_of(tok_ref, b, group):
    return tok_ref[b, 128 * group : 128 * group + 128, :]


def cotangent_of(cot_ref, b, group):
    at = 128 * group
    return cot_ref[b, at : at + 128, :], cot_ref[b, at + 256 : at + 384, :]


def skip_row(place_ref, skip_ref, group):
    at = 4 * (2 * place_ref[1] + place_ref[2]) + 2 * group
    lane = lax.broadcasted_iota(jnp.int32, (1, LANES), 1)
    return jnp.where(lane < HALF, skip_ref[at], skip_ref[at + 1])


def update(c, scale, carry, vector, values):
    return scale * carry + tn(down(vector, vector), down(*parts(values)))


def load(pairs, sems):
    copies = [pltpu.make_async_copy(a, b, sems.at[i]) for i, (a, b) in enumerate(pairs)]
    for one in copies:
        one.start()
    for one in copies:
        one.wait()


def over_blocks(step, kind):
    lax.fori_loop(0, BLOCKS, lambda i, _: step(i), None, unroll=UNROLL[kind])


def pack_kernel(
    u_any, d1_any, d2_any, w1, r1, w2, r2, o1_any, o2_any, cot_any, out_ref, u_ref, d_ref, v_ref, o_ref, cot_ref, sems
):
    load(
        [(cot_any, cot_ref), (u_any, u_ref), (d1_any, d_ref.at[0]), (d2_any, d_ref.at[1])]
        + [(ref, v_ref.at[k]) for k, ref in enumerate((w1, r1, w2, r2))]
        + [(o1_any, o_ref.at[0]), (o2_any, o_ref.at[1])],
        sems,
    )
    lane = lax.broadcasted_iota(jnp.int32, (1, LANES), 1)
    row_flip = one_where(jnp.bitwise_and(o_ref[0], COLS - 1) != jnp.bitwise_and(lane, COLS - 1))
    col_flip = one_where(
        lax.shift_right_logical(o_ref[1], COLS.bit_length() - 1) != jnp.bitwise_and(lane, ROWS - 1)
    )
    flags = down(row_flip, col_flip, jnp.zeros((14, LANES), f32)).astype(bf16)
    for dest in range(8):
        x, core = dest // 2, dest % 2
        at = core * (PART_ROWS + SHARED_ROWS)
        for group in range(2):
            lanes = slice((2 * dest + group) * LANES, (2 * dest + group + 1) * LANES)
            row = at + 128 * group
            out_ref[x, row : row + 128, :] = u_ref[:, lanes]
            hi, lo = parts(cot_ref[:, lanes])
            row += TOKEN_ROWS
            out_ref[x, row : row + 128, :] = hi
            out_ref[x, row + 256 : row + 384, :] = lo
        decays = down(*(d_ref[layer, 4 * dest : 4 * dest + 4, :] for layer in range(2)))
        hi, lo = parts(decays)
        out_ref[x, at + 256 : at + 272, :] = down(hi.astype(f32), lo.astype(f32)).astype(bf16)
    for x in range(4):
        for k in range(4):
            at = PART_ROWS + 128 * k
            out_ref[x, at : at + 128, :] = v_ref[k]
        out_ref[x, PART_ROWS + 512 : PART_ROWS + 528, :] = flags


def gather_kernel(
    place_ref, own, other, tok_ref, cot_ref, sh_ref, ends_ref, rows_ref, run_ref, s_ref, a_ref, sems
):
    z, core = place_ref[0], place_ref[2]
    mine = pl.multiple_of(core * (PART_ROWS + SHARED_ROWS), 16)
    part = pl.multiple_of(core * SHARED_ROWS, 16)
    share = pl.multiple_of((1 - core) * PART_ROWS, 16)
    pairs = []
    for x in range(4):
        near, far = 2 * x + core, 2 * x + 1 - core
        pairs += [
            (own.at[x, pl.ds(mine, TOKEN_ROWS)], tok_ref.at[near]),
            (own.at[x, pl.ds(mine + TOKEN_ROWS, COT_ROWS)], cot_ref.at[near]),
            (own.at[x, pl.ds(PART_ROWS, SHARED_ROWS)], sh_ref.at[near]),
            (other.at[x, pl.ds(part, TOKEN_ROWS)], tok_ref.at[far]),
            (other.at[x, pl.ds(part + TOKEN_ROWS, COT_ROWS)], cot_ref.at[far]),
            (other.at[x, pl.ds(share, SHARED_ROWS)], sh_ref.at[far]),
        ]
    load(pairs, sems)
    c = constants()
    running, layers = decay_rows_of(tok_ref)
    run_ref[...] = running
    for k in range(2):
        rows_ref[k] = layers[k]
    s_ref[...] = jnp.zeros_like(s_ref)
    a_ref[...] = jnp.zeros_like(a_ref)

    def step(i):
        b = i
        writes, _ = vectors(sh_ref, b, 0)
        for group, (left, total) in enumerate(decay_scales(c, rows_ref, b, 0, "left")):
            u = inputs_of(tok_ref, b, group).astype(f32)
            s_ref[group] = update(c, total, s_ref[group], writes, u * left)
        b = BLOCKS - 1 - i
        _, reads = vectors(sh_ref, b, 1)
        for group, (grown, total) in enumerate(decay_scales(c, rows_ref, b, 1, "grown")):
            hi, lo = cotangent_of(cot_ref, b, group)
            dy = hi.astype(f32) + lo.astype(f32)
            a_ref[group] = update(c, total, a_ref[group], reads, dy * grown)

    over_blocks(step, "gather")
    ends_ref[...] = jnp.where(z == 0, s_ref[...], a_ref[...])


def pick_second(source, out_ref, sems):
    load([(source.at[1, x], out_ref.at[x]) for x in range(4)], sems)


def first_forward(place_ref, skip_ref, rows_ref, run_ref, tok_ref, sh_ref, ends_ref, keep_ref, send_ref, state_ref, s_ref):
    z = place_ref[0]
    c = constants()
    s_ref[...] = jnp.where(z == 1, ends_ref[...], 0.0)

    def step(b):
        writes, reads = vectors(sh_ref, b, 0)
        scores = nt(reads, writes)
        turn = mirror(c, sh_ref, b, 0)
        for group, (decay_a, decay_b, grown, left, total) in enumerate(
            decay_block(c, rows_ref, run_ref, b, 0)
        ):
            u = inputs_of(tok_ref, b, group)
            mixed = across(*parts(across(decay_a * scores, decay_b * scores)))
            state = s_ref[group]
            state_both = down(*parts(state))
            state_ref[b, group] = state_both
            u32 = u.astype(f32)
            heads = by_head(c, u)
            y = (
                nn(mixed, down(heads, heads))
                + grown * nn(across(reads, reads), state_both)
                + skip_row(place_ref, skip_ref, group) * u32
            )
            s_ref[group] = update(c, total, state, writes, u32 * left)
            grid = nn(turn, y.astype(bf16)).astype(bf16)
            for k in range(4):
                near, far = grid[32 * k : 32 * k + 16], grid[32 * k + 16 : 32 * k + 32]
                at = pl.multiple_of(64 * b + 16 * k, 16)
                keep_ref[group, pl.ds(at, 16), :] = jnp.where(z == 0, near, far)
                send_ref[group, pl.ds(at, 16), :] = jnp.where(z == 0, far, near)

    over_blocks(step, "first")


def first_backward(place_ref, skip_ref, rows_ref, run_ref, sh_ref, cot_ref, ends_ref, keep_ref, send_ref, adjoint_ref, a_ref):
    z = place_ref[0]
    c = constants()
    a_ref[...] = jnp.where(z == 0, ends_ref[...], 0.0)

    def step(i):
        b = BLOCKS - 1 - i
        writes, reads = vectors(sh_ref, b, 1)
        scores = nt(reads, writes)
        turn = mirror(c, sh_ref, b, 1)
        for group, (decay_a, decay_b, grown, left, total) in enumerate(
            decay_block(c, rows_ref, run_ref, b, 1)
        ):
            hi, lo = cotangent_of(cot_ref, b, group)
            mixed, mixed_low = parts(down(decay_a * scores, decay_b * scores))
            adjoint = a_ref[group]
            adjoint_both = down(*parts(adjoint))
            adjoint_ref[b, group] = adjoint_both
            dy = hi.astype(f32) + lo.astype(f32)
            hi_heads, lo_heads = by_head(c, hi), by_head(c, lo)
            du = (
                tn(down(mixed, mixed_low, mixed), down(hi_heads, hi_heads, lo_heads))
                + left * nn(across(writes, writes), adjoint_both)
                + skip_row(place_ref, skip_ref, group) * dy
            )
            a_ref[group] = update(c, total, adjoint, reads, dy * grown)
            grid = nn(turn, du.astype(bf16)).astype(bf16)
            for k in range(2):
                near, far = grid[64 * k : 64 * k + 32], grid[64 * k + 32 : 64 * k + 64]
                at = pl.multiple_of(64 * b + 32 * k, 32)
                keep_ref[group, pl.ds(at, 32), :] = jnp.where(z == 0, near, far)
                send_ref[group, pl.ds(at, 32), :] = jnp.where(z == 0, far, near)

    over_blocks(step, "first")


def regrid_forward(
    place_ref, rows_ref, sh_ref, cot_ref, keep_ref, got_ref, u2_ref, s_ref, skip_ref, grid_ref
):
    z = place_ref[0]
    c = constants()
    grid_ref[z] = keep_ref[...].astype(f32)
    grid_ref[1 - z] = got_ref[...].astype(f32)
    s_ref[...] = jnp.zeros_like(s_ref)
    skip_ref[...] = jnp.zeros_like(skip_ref)

    def step(b):
        writes, _ = vectors(sh_ref, b, 1)
        turn = mirror(c, sh_ref, b, 1)
        scale = decay_scales(c, rows_ref, b, 1, "left")
        for group in range(2):
            picked = down(
                *(
                    grid_ref[part, group, pl.ds(2 * b + k, 32, stride=16), :]
                    for k in range(2)
                    for part in range(2)
                )
            )
            u32 = nn(turn, picked.astype(bf16))
            u2_ref[b, group] = u32.astype(bf16)
            left, total = scale[group]
            s_ref[group] = update(c, total, s_ref[group], writes, u32 * left)
            hi, lo = cotangent_of(cot_ref, b, group)
            dy = hi.astype(f32) + lo.astype(f32)
            skip_ref[group : group + 1, :] += jnp.sum(u32 * dy, axis=0, keepdims=True)

    over_blocks(step, "regrid")


def regrid_backward(
    place_ref, rows_ref, tok_ref, sh_ref, keep_ref, got_ref, skip_two_ref, _, dy1_ref, ends_ref, grid_ref, skip_ref, a_ref
):
    z = place_ref[0]
    c = constants()
    grid_ref[z] = keep_ref[...].astype(f32)
    grid_ref[1 - z] = got_ref[...].astype(f32)
    a_ref[...] = jnp.zeros_like(a_ref)
    skip_ref[0:2, :] = jnp.zeros((2, LANES), f32)
    skip_ref[2:8, :] = skip_two_ref[0:6, :]

    def step(i):
        b = BLOCKS - 1 - i
        _, reads = vectors(sh_ref, b, 0)
        turn = mirror(c, sh_ref, b, 0)
        scale = decay_scales(c, rows_ref, b, 0, "grown")
        for group in range(2):
            picked = down(
                *(
                    grid_ref[part, group, pl.ds(4 * b + k, 16, stride=32), :]
                    for k in range(4)
                    for part in range(2)
                )
            )
            dy = nn(turn, picked.astype(bf16))
            dy1_ref[b, group] = dy.astype(bf16)
            grown, total = scale[group]
            a_ref[group] = update(c, total, a_ref[group], reads, dy * grown)
            u = inputs_of(tok_ref, b, group).astype(f32)
            skip_ref[group : group + 1, :] += jnp.sum(u * dy, axis=0, keepdims=True)

    over_blocks(step, "regrid")
    for group in range(2):
        ends_ref[LANES * group : LANES * (group + 1), :] = a_ref[group]
    ends_ref[2 * LANES :, :] = skip_ref[...]


def block_gradients(c, rows_ref, run_ref, sh_ref, b, layer, u_of, dy_of, state_of, adjoint_of):
    writes, reads = vectors(sh_ref, b, layer)
    reads_two, writes_two = down(reads, reads), down(writes, writes)
    scores = nt(reads, writes)
    d_scores, d_writes, d_reads = 0.0, 0.0, 0.0
    decay_rows, kept = [], []
    for group, (decay_a, decay_b, grown, left, total) in enumerate(
        decay_block(c, rows_ref, run_ref, b, layer)
    ):
        u, (dy, dy_low) = u_of(group), dy_of(group)
        u32, dy32 = u.astype(f32), dy.astype(f32)
        dy_heads = by_head(c, dy)
        if dy_low is None:
            pairs = nt(dy_heads, u)
        else:
            pairs = nt(across(dy_heads, by_head(c, dy_low)), across(u, u))
            dy32 = dy32 + dy_low.astype(f32)
        pair_a, pair_b = decay_a * pairs[:BLOCK], decay_b * pairs[BLOCK:]
        d_scores = d_scores + pair_a + pair_b
        u_left, dy_grown = u32 * left, dy32 * grown
        u_hi, u_lo = parts(u_left)
        dy_hi, dy_lo = parts(dy_grown)
        state, adjoint = state_of(group), adjoint_of(group)
        read_state = nn(across(reads, reads), state)
        write_adjoint = nn(across(writes, writes), adjoint)
        state_hi, adjoint_hi = state[:LANES], adjoint[:LANES]
        d_writes = (
            d_writes
            + nt(across(u_hi, u_lo), across(adjoint_hi, adjoint_hi))
        )
        d_reads = (
            d_reads
            + nt(across(dy_hi, dy_lo), across(state_hi, state_hi))
        )
        crossing = across((pair_a * scores).astype(bf16), (pair_b * scores).astype(bf16))
        inner = tn(crossing, c["lower_bf"])
        products = down(
            (dy_grown * read_state).astype(bf16),
            (u_left * write_adjoint).astype(bf16),
            (total * (state_hi.astype(f32) * adjoint_hi.astype(f32))).astype(bf16),
        )
        outer = tn(products, c["sums"])
        for k in range(2):
            decay_rows.append(
                jnp.sum(c["before"] * inner[BLOCK * k : BLOCK * (k + 1)], axis=0, keepdims=True)
                + jnp.sum(outer[HALF * k : HALF * (k + 1)], axis=0, keepdims=True)
            )
        kept.append(
            {
                "total": total,
                "left": left,
                "u_left": down(u_hi, u_lo),
                "dy_grown": down(dy_hi, dy_lo),
                "write_adjoint": write_adjoint,
                "dy_heads": dy_heads,
                "dy": dy32,
                "mixed": lambda a=decay_a, h=decay_b: down(
                    (a * scores).astype(bf16), (h * scores).astype(bf16)
                ),
            }
        )
    low = parts(d_scores)
    d_writes = d_writes + tn(down(*low), reads_two)
    d_reads = d_reads + nn(across(*low), writes_two)
    return d_writes, d_reads, down(*decay_rows), kept, writes_two, reads_two


def put_gradients(out_ref, core, b, at, d_writes, d_reads, rows):
    slot, x = jnp.bitwise_xor(b % 2, core), b // 2
    out_ref[slot, x, at : at + 128, :] = d_writes.astype(bf16)
    out_ref[slot, x, at + 128 : at + 256, :] = d_reads.astype(bf16)
    hi, lo = parts(rows)
    small = down(hi.astype(f32), lo.astype(f32), jnp.zeros((8, LANES), f32))
    out_ref[slot, x, at + 256 : at + 272, :] = small.astype(bf16)


def second_forward(place_ref, rows_ref, run_ref, sh_ref, cot_ref, u2_ref, adjoint_ref, ends_ref, out_ref, s_ref):
    core = place_ref[2]
    c = constants()
    s_ref[...] = ends_ref[...]

    def step(b):
        d_writes, d_reads, rows, kept, writes_two, _ = block_gradients(
            c,
            rows_ref,
            run_ref,
            sh_ref,
            b,
            1,
            lambda g: u2_ref[b, g],
            lambda g: cotangent_of(cot_ref, b, g),
            lambda g: down(*parts(s_ref[g])),
            lambda g: adjoint_ref[b, g],
        )
        put_gradients(out_ref, core, b, 0, d_writes, d_reads, rows)
        for group in range(2):
            k = kept[group]
            s_ref[group] = k["total"] * s_ref[group] + tn(writes_two, k["u_left"])

    over_blocks(step, "second")


def second_backward(
    place_ref, skip_ref, rows_ref, run_ref, tok_ref, sh_ref, dy1_ref, state_ref, ends_ref, own_ref, _second, out_ref, sums_ref, a_ref
):
    core = place_ref[2]
    c = constants()
    for group in range(2):
        arrived = ends_ref[LANES * group : LANES * (group + 1), :]
        a_ref[group] = jnp.where(place_ref[0] == 0, arrived, 0.0)
    total = own_ref[2 * LANES :, :] + ends_ref[2 * LANES :, :]
    for k in range(sums_ref.shape[0]):
        sums_ref[k] = total

    def step(i):
        b = BLOCKS - 1 - i
        d_writes, d_reads, rows, kept, _, reads_two = block_gradients(
            c,
            rows_ref,
            run_ref,
            sh_ref,
            b,
            0,
            lambda g: inputs_of(tok_ref, b, g),
            lambda g: (dy1_ref[b, g], None),
            lambda g: state_ref[b, g],
            lambda g: down(*parts(a_ref[g])),
        )
        put_gradients(out_ref, core, b, 256, d_writes, d_reads, rows)
        slot = jnp.bitwise_xor(b % 2, core)
        for group in range(2):
            k = kept[group]
            du = (
                tn(k["mixed"](), k["dy_heads"])
                + k["left"] * k["write_adjoint"]
                + skip_row(place_ref, skip_ref, group) * k["dy"]
            )
            out_ref[slot, b // 2, 128 * group : 128 * group + 128, :] = du.astype(bf16)
            a_ref[group] = k["total"] * a_ref[group] + tn(reads_two, k["dy_grown"])

    over_blocks(step, "second")


def pair_kernel(own_ref, other_ref, own_two_ref, other_two_ref, skip_ref, skip_other_ref, out_ref):
    skips = []
    for ref in (skip_ref, skip_other_ref):
        total = ref[0, 0:4, :]
        for k in range(1, ref.shape[0]):
            total = total + ref[k, 0:4, :]
        hi = total.astype(bf16).astype(f32)
        mid, low = parts(total - hi)
        skips.append(down(hi, mid.astype(f32), low.astype(f32), jnp.zeros((4, LANES), f32)))
    skips = down(*skips).astype(bf16)
    for x in range(4):
        out_ref[x, 0:256, :] = own_ref[0, x, 0:256, :]
        out_ref[x, 256:512, :] = other_ref[x, 0:256, :]
        out_ref[x, 512:768, :] = (
            own_ref[0, x, 256:512, :].astype(f32) + other_ref[x, 256:512, :].astype(f32)
        ).astype(bf16)
        out_ref[x, 768:784, :] = own_ref[0, x, 512:528, :]
        out_ref[x, 784:800, :] = other_ref[x, 512:528, :]
        out_ref[x, 800:832, :] = skips
        out_ref[x, 832:1088, :] = (
            own_two_ref[0, x, 0:256, :].astype(f32) + other_two_ref[x, 0:256, :].astype(f32)
        ).astype(bf16)
        out_ref[x, 1088:1104, :] = own_two_ref[0, x, 256:272, :]
        out_ref[x, 1104:1120, :] = other_two_ref[x, 256:272, :]


def last_kernel(place_ref, back_ref, grad_ref, w1, r1, w2, r2, decay1_ref, decay2_ref, skip_ref):
    core = place_ref[2]

    def chosen(ref, x, at, size, owner):
        near, far = ref[x, at : at + size, :], ref[x, at + size : at + 2 * size, :]
        return jnp.where(core == owner, near, far)

    for x in range(4):
        for owner in range(2):
            both = chosen(back_ref, x, 0, 256, owner)
            for group in range(2):
                at = ((2 * x + owner) * 2 + group) * LANES
                grad_ref[:, at : at + LANES] = both[128 * group : 128 * group + 128]
            at = (2 * x + owner) * 4
            small = chosen(back_ref, x, 768, 16, owner).astype(f32)
            decay1_ref[at : at + 4, :] = small[0:4] + small[4:8]
            small = chosen(back_ref, x, 1088, 16, owner).astype(f32)
            decay2_ref[at : at + 4, :] = small[0:4] + small[4:8]
            small = chosen(back_ref, x, 800, 16, owner).astype(f32)
            skip_ref[at : at + 4, :] = small[0:4] + small[4:8] + small[8:12]
    for ref, at in ((w1, 512), (r1, 640), (w2, 832), (r2, 960)):
        total = back_ref[0, at : at + 128, :].astype(f32)
        for x in range(1, 4):
            total = total + back_ref[x, at : at + 128, :].astype(f32)
        ref[...] = total.astype(bf16)


def call(kernel, outs, scratch, *args, scalars=1, anywhere=(), copies=0, us=5, mib=12):
    shapes = [jax.ShapeDtypeStruct(s, d) for s, d in outs]
    many = len(shapes) > 1
    in_specs = [
        pl.BlockSpec(
            memory_space=pltpu.SMEM if i < scalars else pl.ANY if i in anywhere else pltpu.VMEM
        )
        for i in range(len(args))
    ]
    out_specs = [pl.BlockSpec(memory_space=pltpu.VMEM)] * len(shapes)
    scratch = [pltpu.VMEM(s, d) for s, d in scratch]
    if copies:
        scratch.append(pltpu.SemaphoreType.DMA((copies,)))
    return pl.pallas_call(
        kernel,
        out_shape=shapes if many else shapes[0],
        in_specs=in_specs,
        out_specs=out_specs if many else out_specs[0],
        scratch_shapes=scratch,
        cost_estimate=pl.CostEstimate(flops=us * 10**9, bytes_accessed=10**6, transcendentals=0),
        compiler_params=pltpu.CompilerParams(vmem_limit_bytes=mib * 2**20),
        name=kernel.__name__,
    )(*args)


def pick_slot(values):
    out = (values.shape[1:], bf16)
    return call(pick_second, [out], [], values, scalars=0, anywhere=(0,), copies=4, us=1)


def swap(values, axis):
    return lax.ppermute(values, axis, [(0, 1), (1, 0)])


def over_x(values):
    return lax.all_to_all(values, "x", split_axis=0, concat_axis=0, tiled=True)


def on_device(
    layer_input,
    writes_first,
    reads_first,
    decay_first,
    skip_first,
    writes_second,
    reads_second,
    decay_second,
    skip_second,
    order_first,
    order_second,
    cotangent,
):
    length, features = layer_input.shape[1:]
    head_count = skip_first.shape[0]
    head_size = features // head_count
    z, x, core = (lax.axis_index(a) for a in ("z", "x", "core"))
    place = jnp.stack([z, x, core]).astype(jnp.int32)

    own = over_x(
        call(
            pack_kernel,
            [((4, SEND_ROWS, LANES), bf16)],
            [
                ((length, features), bf16),
                ((2, head_count, length), f32),
                ((4, length, LANES), bf16),
                ((2, 1, length), jnp.int32),
                ((length, features), f32),
            ],
            layer_input[0],
            decay_first[0],
            decay_second[0],
            writes_first[0],
            reads_first[0],
            writes_second[0],
            reads_second[0],
            order_first.reshape(1, length),
            order_second.reshape(1, length),
            cotangent[0],
            scalars=0,
            anywhere=range(10),
            mib=60,
            copies=10,
            us=2,
        )
    )
    theirs = lax.dynamic_slice_in_dim(own, (1 - core) * PART_ROWS, PART_ROWS + SHARED_ROWS, axis=1)
    other = swap(theirs, "core")

    carry = ((2, LANES, LANES), f32)
    saved = ((BLOCKS, 2, 2 * LANES, LANES), bf16)
    half_grid = ((2, 512, LANES), bf16)
    block = ((BLOCKS, 2, BLOCK, LANES), bf16)
    grids = ((2, 2, 512, LANES), f32)
    few = ((8, LANES), f32)

    tok, cot, sh, end, rows, run = call(
        gather_kernel,
        [
            ((BLOCKS, TOKEN_ROWS, LANES), bf16),
            ((BLOCKS, COT_ROWS, LANES), bf16),
            ((BLOCKS, SHARED_ROWS, LANES), bf16),
            carry,
            ((2, BLOCKS, 32, LANES), bf16),
            ((BLOCKS, 8, LANES), f32),
        ],
        [carry, carry],
        place,
        own,
        other,
        anywhere=(1, 2),
        copies=24,
    )
    end = swap(end, "z")
    keep, send, states = call(
        first_forward,
        [half_grid, half_grid, saved],
        [carry],
        place,
        skip_first,
        rows,
        run,
        tok,
        sh,
        end,
        scalars=2,
    )
    got = swap(send, "z")
    keep_back, send_back, adjoints = call(
        first_backward,
        [half_grid, half_grid, saved],
        [carry],
        place,
        skip_second,
        rows,
        run,
        sh,
        cot,
        end,
        scalars=2,
    )
    got_back = swap(send_back, "z")
    u2, end, skip_two = call(
        regrid_forward, [block, carry, few], [grids], place, rows, sh, cot, keep, got
    )
    end = lax.ppermute(end, "z", [(0, 1)])
    dy1, end_own = call(
        regrid_backward,
        [block, ((2 * LANES + 8, LANES), f32)],
        [grids, few, carry],
        place,
        rows,
        tok,
        sh,
        keep_back,
        got_back,
        skip_two,
        end,
        anywhere=(7,),
    )
    end_back = swap(end_own, "z")

    out_two = call(
        second_forward,
        [((2, 4, 272, LANES), bf16)],
        [carry],
        place,
        rows,
        run,
        sh,
        cot,
        u2,
        adjoints,
        end,
        us=8,
    )
    clips = lax.axis_size("dp")
    out, skip_sums = call(
        second_backward,
        [((2, 4, 528, LANES), bf16), ((clips, 8, LANES), f32)],
        [carry],
        place,
        skip_first,
        rows,
        run,
        tok,
        sh,
        dy1,
        states,
        end_back,
        end_own,
        out_two,
        scalars=2,
        anywhere=(10,),
        us=8,
    )
    skip_sums = lax.all_to_all(skip_sums, "dp", split_axis=0, concat_axis=0, tiled=True)
    back = over_x(
        call(
            pair_kernel,
            [((4, 1120, LANES), bf16)],
            [],
            out,
            swap(pick_slot(out), "core"),
            out_two,
            swap(pick_slot(out_two), "core"),
            skip_sums,
            swap(skip_sums, "core"),
            scalars=0,
            us=1,
        )
    )
    vector = ((length, LANES), bf16)
    decay = ((head_count, length), f32)
    grad_input, w1, r1, w2, r2, decay1, decay2, skip_lanes = call(
        last_kernel,
        [((length, features), bf16), vector, vector, vector, vector, decay, decay, ((head_count, LANES), f32)],
        [],
        place,
        back,
        us=1,
    )
    seq_count = lax.axis_size("z") * lax.axis_size("x") * lax.axis_size("core")
    factor = 1.0 / math.sqrt(clips * seq_count * length * head_size)
    skip_grads = skip_lanes.reshape(8, 2, 2, 2, head_size).sum(-1)
    skip_grads = skip_grads.transpose(1, 0, 2, 3).reshape(2, head_count) * factor
    return (
        grad_input[None],
        w1[None],
        r1[None],
        decay1[None],
        skip_grads[0],
        w2[None],
        r2[None],
        decay2[None],
        skip_grads[1],
    )


def solution(mesh):
    finer = Mesh(mesh.devices.reshape(-1, 2, 4, 2), ("dp", "z", "x", "core"))
    seq = ("z", "x", "core")
    by_token, by_decay = P("dp", seq, None), P("dp", None, seq)
    return jax.shard_map(
        on_device,
        mesh=finer,
        in_specs=(
            by_token,
            by_token,
            by_token,
            by_decay,
            P(),
            by_token,
            by_token,
            by_decay,
            P(),
            P(seq),
            P(seq),
            by_token,
        ),
        out_specs=(
            by_token,
            by_token,
            by_token,
            by_decay,
            P(),
            by_token,
            by_token,
            by_decay,
            P(),
        ),
        check_vma=False,
    )
```

```python
import math

import jax
import jax.numpy as jnp
from jax import lax
from jax.experimental import pallas as pl
from jax.experimental.pallas import tpu as pltpu
from jax.sharding import Mesh
from jax.sharding import PartitionSpec as P

COLS = 32
ROWS = 64
BLOCK = 128
HALF = 64
LANES = 128
PART_ROWS = 784
TOKEN_ROWS = 272
SHARED_ROWS = 528
SEND_ROWS = 2 * PART_ROWS + SHARED_ROWS
COT_ROWS = 512
BLOCKS = 8
SKIP_SCALE = 1.0 / math.sqrt(16 * 2048 * 64)
UNROLL = {"gather": 8, "first": 4, "regrid": 8, "second": 4}

f32 = jnp.float32
bf16 = jnp.bfloat16


def nn(a, b):
    return lax.dot_general(a, b, (((1,), (0,)), ((), ())), preferred_element_type=f32)


def nt(a, b):
    return lax.dot_general(a, b, (((1,), (1,)), ((), ())), preferred_element_type=f32)


def tn(a, b):
    return lax.dot_general(a, b, (((0,), (0,)), ((), ())), preferred_element_type=f32)


def down(*values):
    return jnp.concatenate(values, axis=0)


def across(*values):
    return jnp.concatenate(values, axis=1)


def parts(values):
    hi = values.astype(bf16)
    return hi, (values - hi.astype(f32)).astype(bf16)


def iota(dim):
    return lax.broadcasted_iota(jnp.int32, (BLOCK, BLOCK), dim)


def one_where(cond):
    return jnp.where(cond, f32(1.0), f32(0.0))


def constants():
    row, col = iota(0), iota(1)
    lower = one_where(col <= row)
    before = one_where(row < col)
    head_a = one_where(col < HALF)
    head_b = 1.0 - head_a
    return {
        "head_a": head_a.astype(bf16),
        "head_b": head_b.astype(bf16),
        "causal": col <= row,
        "lower_bf": lower.astype(bf16),
        "grown": spread_matrix(12, 4, 2, HALF),
        "left": spread_matrix(20, 4, 2, HALF),
        "all": across(
            spread_matrix(0, 4, 3, LANES), spread_matrix(12, 4, 2, HALF), spread_matrix(20, 4, 2, HALF)
        ),
        "before": before,
        "sums": down(lower, before, jnp.ones((BLOCK, BLOCK), f32)).astype(bf16),
        "same": one_where(row == col),
        "mirror_row": one_where(row + col == 2 * (row - row % COLS) + COLS - 1),
        "mirror_col": one_where(row + col == 2 * (row - row % ROWS) + ROWS - 1),
    }


def decay_rows_of(tok_ref):
    small = down(*(tok_ref[b, 256:272, :] for b in range(BLOCKS)))
    row, col = iota(0), iota(1)
    sums = nn(small, one_where(row <= col).astype(bf16)).reshape(BLOCKS, 16, LANES)
    running = sums[:, 0:8] + sums[:, 8:16]
    hi = running.astype(bf16).astype(f32)
    mid = (running - hi).astype(bf16).astype(f32)
    grown = jnp.exp(running)
    left = jnp.exp(running[:, :, LANES - 1 :] - running)
    grown_hi, left_hi = grown.astype(bf16).astype(f32), left.astype(bf16).astype(f32)
    pieces = (hi, mid, running - hi - mid, grown_hi, grown - grown_hi, left_hi, left - left_hi)
    zeros = jnp.zeros((BLOCKS, 4, LANES), f32)
    layers = [
        jnp.concatenate([p[:, 4 * k : 4 * k + 4] for p in pieces] + [zeros], axis=1) for k in range(2)
    ]
    return running, [one.astype(bf16) for one in layers]


def spread_matrix(first, count, copies, width):
    row = lax.broadcasted_iota(jnp.int32, (32, count * width), 0)
    col = lax.broadcasted_iota(jnp.int32, (32, count * width), 1)
    inside = (row >= first) & (row < first + copies * count)
    return one_where(inside & ((row - first) % count == col // width)).astype(bf16)


def decay_scales(c, rows_ref, b, layer, which):
    rows = rows_ref[layer, b]
    values = tn(rows, c[which])
    if which == "grown":
        total = values[BLOCK - 1 :, :]
    else:
        total = tn(rows, c["grown"])[BLOCK - 1 :, :]
    return [(values[:, LANES * g : LANES * g + LANES], total[:, LANES * g : LANES * g + LANES]) for g in range(2)]


def decay_block(c, rows_ref, run_ref, b, layer):
    rows = rows_ref[layer, b]
    values = tn(rows, c["all"])
    running = run_ref[b]
    decays = [
        jnp.where(
            c["causal"],
            jnp.exp(
                jnp.minimum(
                    values[:, LANES * k : LANES * k + LANES] - running[4 * layer + k : 4 * layer + k + 1], 0.0
                )
            ),
            0.0,
        )
        for k in range(4)
    ]
    both = []
    for g in range(2):
        grown = values[:, 512 + LANES * g : 640 + LANES * g]
        left = values[:, 768 + LANES * g : 896 + LANES * g]
        both.append((decays[2 * g], decays[2 * g + 1], grown, left, grown[BLOCK - 1 :, :]))
    return both


def by_head(c, values):
    return down(values * c["head_a"], values * c["head_b"])


def mirror(c, sh_ref, b, layer):
    flags = sh_ref[b, 512:528, :].astype(f32)[layer : layer + 1]
    turned = c["mirror_col"] if layer else c["mirror_row"]
    return (flags * turned + (1.0 - flags) * c["same"]).astype(bf16)


def vectors(sh_ref, b, layer):
    at = 256 * layer
    return sh_ref[b, at : at + 128, :], sh_ref[b, at + 128 : at + 256, :]


def inputs_of(tok_ref, b, group):
    return tok_ref[b, 128 * group : 128 * group + 128, :]


def cotangent_of(cot_ref, b, group):
    at = 128 * group
    return cot_ref[b, at : at + 128, :], cot_ref[b, at + 256 : at + 384, :]


def skip_row(place_ref, skip_ref, group):
    at = 4 * (2 * place_ref[1] + place_ref[2]) + 2 * group
    lane = lax.broadcasted_iota(jnp.int32, (1, LANES), 1)
    return jnp.where(lane < HALF, skip_ref[at], skip_ref[at + 1])


def update(carry_ref, totals, vector, values):
    halves = [parts(v) if not isinstance(v, tuple) else v for v in values]
    moved = tn(vector, across(halves[0][0], halves[1][0], halves[0][1], halves[1][1]))
    for g in range(2):
        at = LANES * g
        carry_ref[g] = (
            totals[g] * carry_ref[g] + moved[:, at : at + LANES] + moved[:, 2 * LANES + at : 3 * LANES + at]
        )


def update_pair(scale, carry, vector, values):
    return scale * carry + tn(down(vector, vector), down(*parts(values)))


def load(pairs, sems):
    copies = [pltpu.make_async_copy(a, b, sems.at[i]) for i, (a, b) in enumerate(pairs)]
    for one in copies:
        one.start()
    for one in copies:
        one.wait()


def over_blocks(step, kind):
    lax.fori_loop(0, BLOCKS, lambda i, _: step(i), None, unroll=UNROLL[kind])


def pack_kernel(
    u_any, d1_any, d2_any, w1, r1, w2, r2, o1_any, o2_any, cot_any, out_ref, u_ref, d_ref, v_ref, o_ref, cot_ref, sems
):
    load(
        [(cot_any, cot_ref), (u_any, u_ref), (d1_any, d_ref.at[0]), (d2_any, d_ref.at[1])]
        + [(ref, v_ref.at[k]) for k, ref in enumerate((w1, r1, w2, r2))]
        + [(o1_any, o_ref.at[0]), (o2_any, o_ref.at[1])],
        sems,
    )
    lane = lax.broadcasted_iota(jnp.int32, (1, LANES), 1)
    row_flip = one_where(jnp.bitwise_and(o_ref[0], COLS - 1) != jnp.bitwise_and(lane, COLS - 1))
    col_flip = one_where(
        lax.shift_right_logical(o_ref[1], COLS.bit_length() - 1) != jnp.bitwise_and(lane, ROWS - 1)
    )
    flags = down(row_flip, col_flip, jnp.zeros((14, LANES), f32)).astype(bf16)
    for dest in range(8):
        x, core = dest // 2, dest % 2
        at = core * (PART_ROWS + SHARED_ROWS)
        for group in range(2):
            lanes = slice((2 * dest + group) * LANES, (2 * dest + group + 1) * LANES)
            row = at + 128 * group
            out_ref[x, row : row + 128, :] = u_ref[:, lanes]
            hi, lo = parts(cot_ref[:, lanes])
            row += TOKEN_ROWS
            out_ref[x, row : row + 128, :] = hi
            out_ref[x, row + 256 : row + 384, :] = lo
        decays = down(*(d_ref[layer, 4 * dest : 4 * dest + 4, :] for layer in range(2)))
        hi, lo = parts(decays)
        out_ref[x, at + 256 : at + 272, :] = down(hi.astype(f32), lo.astype(f32)).astype(bf16)
    for x in range(4):
        for k in range(4):
            at = PART_ROWS + 128 * k
            out_ref[x, at : at + 128, :] = v_ref[k]
        out_ref[x, PART_ROWS + 512 : PART_ROWS + 528, :] = flags


def gather_kernel(
    place_ref, own, other, tok_ref, cot_ref, sh_ref, ends_ref, rows_ref, run_ref, s_ref, a_ref, sems
):
    z, core = place_ref[0], place_ref[2]
    mine = pl.multiple_of(core * (PART_ROWS + SHARED_ROWS), 16)
    part = pl.multiple_of(core * SHARED_ROWS, 16)
    share = pl.multiple_of((1 - core) * PART_ROWS, 16)
    tokens, vectors_in, cotangents = [], [], []
    for x in range(4):
        near, far = 2 * x + core, 2 * x + 1 - core
        tokens += [
            (own.at[x, pl.ds(mine, TOKEN_ROWS)], tok_ref.at[near]),
            (other.at[x, pl.ds(part, TOKEN_ROWS)], tok_ref.at[far]),
        ]
        vectors_in += [
            (own.at[x, pl.ds(PART_ROWS, SHARED_ROWS)], sh_ref.at[near]),
            (other.at[x, pl.ds(share, SHARED_ROWS)], sh_ref.at[far]),
        ]
        cotangents += [
            (own.at[x, pl.ds(mine + TOKEN_ROWS, COT_ROWS)], cot_ref.at[near]),
            (other.at[x, pl.ds(part + TOKEN_ROWS, COT_ROWS)], cot_ref.at[far]),
        ]
    copies = [
        pltpu.make_async_copy(a, b, sems.at[i])
        for i, (a, b) in enumerate(tokens + vectors_in + cotangents)
    ]
    for one in copies:
        one.start()
    c = constants()
    s_ref[...] = jnp.zeros_like(s_ref)
    a_ref[...] = jnp.zeros_like(a_ref)
    for one in copies[:8]:
        one.wait()
    running, layers = decay_rows_of(tok_ref)
    run_ref[...] = running
    for k in range(2):
        rows_ref[k] = layers[k]
    for one in copies[8:16]:
        one.wait()

    def forward(b):
        writes, _ = vectors(sh_ref, b, 0)
        scale = decay_scales(c, rows_ref, b, 0, "left")
        values = [inputs_of(tok_ref, b, g).astype(f32) * scale[g][0] for g in range(2)]
        update(s_ref, [one[1] for one in scale], writes, values)

    def backward(i):
        b = BLOCKS - 1 - i
        _, reads = vectors(sh_ref, b, 1)
        scale = decay_scales(c, rows_ref, b, 1, "grown")
        values = []
        for group in range(2):
            hi, lo = cotangent_of(cot_ref, b, group)
            values.append((hi.astype(f32) + lo.astype(f32)) * scale[group][0])
        update(a_ref, [one[1] for one in scale], reads, values)

    over_blocks(forward, "gather")
    for one in copies[16:]:
        one.wait()
    over_blocks(backward, "gather")
    ends_ref[...] = jnp.where(z == 0, s_ref[...], a_ref[...])


def pick_second(source, out_ref, sems):
    load([(source.at[1, x], out_ref.at[x]) for x in range(4)], sems)


def first_forward(place_ref, skip_ref, rows_ref, run_ref, tok_ref, sh_ref, ends_ref, keep_ref, send_ref, state_ref, s_ref):
    z = place_ref[0]
    c = constants()
    s_ref[...] = jnp.where(z == 1, ends_ref[...], 0.0)

    def step(b):
        writes, reads = vectors(sh_ref, b, 0)
        scores = nt(reads, writes)
        turn = mirror(c, sh_ref, b, 0)
        for group, (decay_a, decay_b, grown, left, total) in enumerate(
            decay_block(c, rows_ref, run_ref, b, 0)
        ):
            u = inputs_of(tok_ref, b, group)
            mixed = across(*parts(across(decay_a * scores, decay_b * scores)))
            state = s_ref[group]
            state_both = down(*parts(state))
            state_ref[b, group] = state_both
            u32 = u.astype(f32)
            heads = by_head(c, u)
            y = (
                nn(mixed, down(heads, heads))
                + grown * nn(across(reads, reads), state_both)
                + skip_row(place_ref, skip_ref, group) * u32
            )
            s_ref[group] = update_pair(total, state, writes, u32 * left)
            grid = nn(turn, y.astype(bf16)).astype(bf16)
            for k in range(4):
                near, far = grid[32 * k : 32 * k + 16], grid[32 * k + 16 : 32 * k + 32]
                at = pl.multiple_of(64 * b + 16 * k, 16)
                keep_ref[group, pl.ds(at, 16), :] = jnp.where(z == 0, near, far)
                send_ref[group, pl.ds(at, 16), :] = jnp.where(z == 0, far, near)

    over_blocks(step, "first")


def first_backward(place_ref, skip_ref, rows_ref, run_ref, sh_ref, cot_ref, ends_ref, keep_ref, send_ref, adjoint_ref, a_ref):
    z = place_ref[0]
    c = constants()
    a_ref[...] = jnp.where(z == 0, ends_ref[...], 0.0)

    def step(i):
        b = BLOCKS - 1 - i
        writes, reads = vectors(sh_ref, b, 1)
        scores = nt(reads, writes)
        turn = mirror(c, sh_ref, b, 1)
        for group, (decay_a, decay_b, grown, left, total) in enumerate(
            decay_block(c, rows_ref, run_ref, b, 1)
        ):
            hi, lo = cotangent_of(cot_ref, b, group)
            mixed, mixed_low = parts(down(decay_a * scores, decay_b * scores))
            adjoint = a_ref[group]
            adjoint_both = down(*parts(adjoint))
            adjoint_ref[b, group] = adjoint_both
            dy = hi.astype(f32) + lo.astype(f32)
            hi_heads, lo_heads = by_head(c, hi), by_head(c, lo)
            du = (
                tn(down(mixed, mixed_low, mixed), down(hi_heads, hi_heads, lo_heads))
                + left * nn(across(writes, writes), adjoint_both)
                + skip_row(place_ref, skip_ref, group) * dy
            )
            a_ref[group] = update_pair(total, adjoint, reads, dy * grown)
            grid = nn(turn, du.astype(bf16)).astype(bf16)
            for k in range(2):
                near, far = grid[64 * k : 64 * k + 32], grid[64 * k + 32 : 64 * k + 64]
                at = pl.multiple_of(64 * b + 32 * k, 32)
                keep_ref[group, pl.ds(at, 32), :] = jnp.where(z == 0, near, far)
                send_ref[group, pl.ds(at, 32), :] = jnp.where(z == 0, far, near)

    over_blocks(step, "first")


def regrid_forward(
    place_ref, rows_ref, sh_ref, cot_ref, keep_ref, got_ref, u2_ref, s_ref, skip_ref, grid_ref
):
    z = place_ref[0]
    c = constants()
    grid_ref[z] = keep_ref[...].astype(f32)
    grid_ref[1 - z] = got_ref[...].astype(f32)
    s_ref[...] = jnp.zeros_like(s_ref)
    skip_ref[...] = jnp.zeros_like(skip_ref)

    def step(b):
        writes, _ = vectors(sh_ref, b, 1)
        turn = mirror(c, sh_ref, b, 1)
        scale = decay_scales(c, rows_ref, b, 1, "left")
        values = []
        for group in range(2):
            picked = down(
                *(
                    grid_ref[part, group, pl.ds(2 * b + k, 32, stride=16), :]
                    for k in range(2)
                    for part in range(2)
                )
            )
            u32 = nn(turn, picked.astype(bf16))
            u2_ref[b, group] = u32.astype(bf16)
            values.append(u32 * scale[group][0])
            hi, lo = cotangent_of(cot_ref, b, group)
            dy = hi.astype(f32) + lo.astype(f32)
            skip_ref[group : group + 1, :] += jnp.sum(u32 * dy, axis=0, keepdims=True)
        update(s_ref, [one[1] for one in scale], writes, values)

    over_blocks(step, "regrid")


def regrid_backward(
    place_ref, rows_ref, tok_ref, sh_ref, keep_ref, got_ref, skip_two_ref, dy1_ref, ends_ref, grid_ref, skip_ref, a_ref
):
    z = place_ref[0]
    c = constants()
    grid_ref[z] = keep_ref[...].astype(f32)
    grid_ref[1 - z] = got_ref[...].astype(f32)
    a_ref[...] = jnp.zeros_like(a_ref)
    skip_ref[0:2, :] = jnp.zeros((2, LANES), f32)
    skip_ref[2:8, :] = skip_two_ref[0:6, :]

    def step(i):
        b = BLOCKS - 1 - i
        _, reads = vectors(sh_ref, b, 0)
        turn = mirror(c, sh_ref, b, 0)
        scale = decay_scales(c, rows_ref, b, 0, "grown")
        values = []
        for group in range(2):
            picked = down(
                *(
                    grid_ref[part, group, pl.ds(4 * b + k, 16, stride=32), :]
                    for k in range(4)
                    for part in range(2)
                )
            )
            dy = nn(turn, picked.astype(bf16))
            dy1_ref[b, group] = dy.astype(bf16)
            values.append(dy * scale[group][0])
            u = inputs_of(tok_ref, b, group).astype(f32)
            skip_ref[group : group + 1, :] += jnp.sum(u * dy, axis=0, keepdims=True)
        update(a_ref, [one[1] for one in scale], reads, values)

    over_blocks(step, "regrid")
    for group in range(2):
        ends_ref[LANES * group : LANES * (group + 1), :] = a_ref[group]
    ends_ref[2 * LANES :, :] = skip_ref[...]


def block_gradients(c, rows_ref, run_ref, sh_ref, b, layer, u_of, dy_of, state_of, adjoint_of):
    writes, reads = vectors(sh_ref, b, layer)
    reads_two, writes_two = down(reads, reads), down(writes, writes)
    scores = nt(reads, writes)
    d_scores, d_writes, d_reads = 0.0, 0.0, 0.0
    decay_rows, kept = [], []
    for group, (decay_a, decay_b, grown, left, total) in enumerate(
        decay_block(c, rows_ref, run_ref, b, layer)
    ):
        u, (dy, dy_low) = u_of(group), dy_of(group)
        u32, dy32 = u.astype(f32), dy.astype(f32)
        dy_heads = by_head(c, dy)
        if dy_low is None:
            pairs = nt(dy_heads, u)
        else:
            pairs = nt(across(dy_heads, by_head(c, dy_low)), across(u, u))
            dy32 = dy32 + dy_low.astype(f32)
        pair_a, pair_b = decay_a * pairs[:BLOCK], decay_b * pairs[BLOCK:]
        d_scores = d_scores + pair_a + pair_b
        u_left, dy_grown = u32 * left, dy32 * grown
        u_hi, u_lo = parts(u_left)
        dy_hi, dy_lo = parts(dy_grown)
        state, adjoint = state_of(group), adjoint_of(group)
        read_state = nn(across(reads, reads), state)
        write_adjoint = nn(across(writes, writes), adjoint)
        state_hi, adjoint_hi = state[:LANES], adjoint[:LANES]
        d_writes = (
            d_writes
            + nt(across(u_hi, u_lo), across(adjoint_hi, adjoint_hi))
        )
        d_reads = (
            d_reads
            + nt(across(dy_hi, dy_lo), across(state_hi, state_hi))
        )
        crossing = across((pair_a * scores).astype(bf16), (pair_b * scores).astype(bf16))
        inner = tn(crossing, c["lower_bf"])
        products = down(
            (dy_grown * read_state).astype(bf16),
            (u_left * write_adjoint).astype(bf16),
            (total * (state_hi.astype(f32) * adjoint_hi.astype(f32))).astype(bf16),
        )
        outer = tn(products, c["sums"])
        for k in range(2):
            decay_rows.append(
                jnp.sum(c["before"] * inner[BLOCK * k : BLOCK * (k + 1)], axis=0, keepdims=True)
                + jnp.sum(outer[HALF * k : HALF * (k + 1)], axis=0, keepdims=True)
            )
        kept.append(
            {
                "total": total,
                "left": left,
                "u_left": down(u_hi, u_lo),
                "dy_grown": down(dy_hi, dy_lo),
                "write_adjoint": write_adjoint,
                "dy_heads": dy_heads,
                "dy": dy32,
                "mixed": lambda a=decay_a, h=decay_b: down(
                    (a * scores).astype(bf16), (h * scores).astype(bf16)
                ),
            }
        )
    low = parts(d_scores)
    d_writes = d_writes + tn(down(*low), reads_two)
    d_reads = d_reads + nn(across(*low), writes_two)
    return d_writes, d_reads, down(*decay_rows), kept, writes_two, reads_two


def put_gradients(out_ref, core, b, at, d_writes, d_reads, rows):
    slot, x = jnp.bitwise_xor(b % 2, core), b // 2
    out_ref[slot, x, at : at + 128, :] = d_writes.astype(bf16)
    out_ref[slot, x, at + 128 : at + 256, :] = d_reads.astype(bf16)
    hi, lo = parts(rows)
    small = down(hi.astype(f32), lo.astype(f32), jnp.zeros((8, LANES), f32))
    out_ref[slot, x, at + 256 : at + 272, :] = small.astype(bf16)


def second_forward(place_ref, rows_ref, run_ref, sh_ref, cot_ref, u2_ref, adjoint_ref, ends_ref, out_ref, s_ref):
    core = place_ref[2]
    c = constants()
    s_ref[...] = ends_ref[...]

    def step(b):
        d_writes, d_reads, rows, kept, writes_two, _ = block_gradients(
            c,
            rows_ref,
            run_ref,
            sh_ref,
            b,
            1,
            lambda g: u2_ref[b, g],
            lambda g: cotangent_of(cot_ref, b, g),
            lambda g: down(*parts(s_ref[g])),
            lambda g: adjoint_ref[b, g],
        )
        put_gradients(out_ref, core, b, 0, d_writes, d_reads, rows)
        for group in range(2):
            k = kept[group]
            s_ref[group] = k["total"] * s_ref[group] + tn(writes_two, k["u_left"])

    over_blocks(step, "second")


def second_backward(
    place_ref, skip_ref, rows_ref, run_ref, tok_ref, sh_ref, dy1_ref, state_ref, ends_ref, own_ref, _second, out_ref, sums_ref, a_ref
):
    core = place_ref[2]
    c = constants()
    for group in range(2):
        arrived = ends_ref[LANES * group : LANES * (group + 1), :]
        a_ref[group] = jnp.where(place_ref[0] == 0, arrived, 0.0)
    total = own_ref[2 * LANES :, :] + ends_ref[2 * LANES :, :]
    for k in range(sums_ref.shape[0]):
        sums_ref[k] = total

    def step(i):
        b = BLOCKS - 1 - i
        d_writes, d_reads, rows, kept, _, reads_two = block_gradients(
            c,
            rows_ref,
            run_ref,
            sh_ref,
            b,
            0,
            lambda g: inputs_of(tok_ref, b, g),
            lambda g: (dy1_ref[b, g], None),
            lambda g: state_ref[b, g],
            lambda g: down(*parts(a_ref[g])),
        )
        put_gradients(out_ref, core, b, 256, d_writes, d_reads, rows)
        slot = jnp.bitwise_xor(b % 2, core)
        for group in range(2):
            k = kept[group]
            du = (
                tn(k["mixed"](), k["dy_heads"])
                + k["left"] * k["write_adjoint"]
                + skip_row(place_ref, skip_ref, group) * k["dy"]
            )
            out_ref[slot, b // 2, 128 * group : 128 * group + 128, :] = du.astype(bf16)
            a_ref[group] = k["total"] * a_ref[group] + tn(reads_two, k["dy_grown"])

    over_blocks(step, "second")


def pair_kernel(own_ref, other_ref, own_two_ref, other_two_ref, skip_ref, skip_other_ref, out_ref):
    skips = []
    for ref in (skip_ref, skip_other_ref):
        total = ref[0, 0:4, :]
        for k in range(1, ref.shape[0]):
            total = total + ref[k, 0:4, :]
        hi = total.astype(bf16).astype(f32)
        mid, low = parts(total - hi)
        skips.append(down(hi, mid.astype(f32), low.astype(f32), jnp.zeros((4, LANES), f32)))
    skips = down(*skips).astype(bf16)
    for x in range(4):
        out_ref[x, 0:256, :] = own_ref[0, x, 0:256, :]
        out_ref[x, 256:512, :] = other_ref[x, 0:256, :]
        out_ref[x, 512:768, :] = (
            own_ref[0, x, 256:512, :].astype(f32) + other_ref[x, 256:512, :].astype(f32)
        ).astype(bf16)
        out_ref[x, 768:784, :] = own_ref[0, x, 512:528, :]
        out_ref[x, 784:800, :] = other_ref[x, 512:528, :]
        out_ref[x, 800:832, :] = skips
        out_ref[x, 832:1088, :] = (
            own_two_ref[0, x, 0:256, :].astype(f32) + other_two_ref[x, 0:256, :].astype(f32)
        ).astype(bf16)
        out_ref[x, 1088:1104, :] = own_two_ref[0, x, 256:272, :]
        out_ref[x, 1104:1120, :] = other_two_ref[x, 256:272, :]


def last_kernel(place_ref, back_ref, grad_ref, w1, r1, w2, r2, decay1_ref, decay2_ref, skip1_ref, skip2_ref):
    core = place_ref[2]

    def chosen(ref, x, at, size, owner):
        near, far = ref[x, at : at + size, :], ref[x, at + size : at + 2 * size, :]
        return jnp.where(core == owner, near, far)

    lanes = []
    for x in range(4):
        for owner in range(2):
            both = chosen(back_ref, x, 0, 256, owner)
            for group in range(2):
                at = ((2 * x + owner) * 2 + group) * LANES
                grad_ref[:, at : at + LANES] = both[128 * group : 128 * group + 128]
            at = (2 * x + owner) * 4
            small = chosen(back_ref, x, 768, 16, owner).astype(f32)
            decay1_ref[at : at + 4, :] = small[0:4] + small[4:8]
            small = chosen(back_ref, x, 1088, 16, owner).astype(f32)
            decay2_ref[at : at + 4, :] = small[0:4] + small[4:8]
            small = chosen(back_ref, x, 800, 16, owner).astype(f32)
            lanes.append(small[0:4] + small[4:8] + small[8:12])
    lanes = down(*lanes)
    row, head = (lax.broadcasted_iota(jnp.int32, (32, 32), k) for k in range(2))
    lane, side = (lax.broadcasted_iota(jnp.int32, (LANES, 32), k) for k in range(2))
    folded = lax.dot_general(
        lanes,
        one_where(lane // HALF == side % 2),
        (((1,), (0,)), ((), ())),
        precision=lax.Precision.HIGHEST,
        preferred_element_type=f32,
    )
    owner = (row // 4 == head // 4) & (row % 2 == head // 2 % 2)
    for layer, ref in enumerate((skip1_ref, skip2_ref)):
        kept = jnp.where(owner & (row // 2 % 2 == layer), folded, 0.0)
        ref[...] = jnp.sum(kept, axis=0, keepdims=True) * SKIP_SCALE
    for ref, at in ((w1, 512), (r1, 640), (w2, 832), (r2, 960)):
        total = back_ref[0, at : at + 128, :].astype(f32)
        for x in range(1, 4):
            total = total + back_ref[x, at : at + 128, :].astype(f32)
        ref[...] = total.astype(bf16)


def call(kernel, outs, scratch, *args, scalars=1, anywhere=(), copies=0, us=5, mib=12):
    shapes = [jax.ShapeDtypeStruct(s, d) for s, d in outs]
    many = len(shapes) > 1
    in_specs = [
        pl.BlockSpec(
            memory_space=pltpu.SMEM if i < scalars else pl.ANY if i in anywhere else pltpu.VMEM
        )
        for i in range(len(args))
    ]
    out_specs = [pl.BlockSpec(memory_space=pltpu.VMEM)] * len(shapes)
    scratch = [pltpu.VMEM(s, d) for s, d in scratch]
    if copies:
        scratch.append(pltpu.SemaphoreType.DMA((copies,)))
    return pl.pallas_call(
        kernel,
        out_shape=shapes if many else shapes[0],
        in_specs=in_specs,
        out_specs=out_specs if many else out_specs[0],
        scratch_shapes=scratch,
        cost_estimate=pl.CostEstimate(flops=us * 10**9, bytes_accessed=10**6, transcendentals=0),
        compiler_params=pltpu.CompilerParams(vmem_limit_bytes=mib * 2**20),
        name=kernel.__name__,
    )(*args)


def pick_slot(values):
    out = (values.shape[1:], bf16)
    return call(pick_second, [out], [], values, scalars=0, anywhere=(0,), copies=4, us=1)


def swap(values, axis):
    return lax.ppermute(values, axis, [(0, 1), (1, 0)])


def over_x(values):
    return lax.all_to_all(values, "x", split_axis=0, concat_axis=0, tiled=True)


def on_device(
    layer_input,
    writes_first,
    reads_first,
    decay_first,
    skip_first,
    writes_second,
    reads_second,
    decay_second,
    skip_second,
    order_first,
    order_second,
    cotangent,
):
    length, features = layer_input.shape[1:]
    head_count = skip_first.shape[0]
    head_size = features // head_count
    z, x, core = (lax.axis_index(a) for a in ("z", "x", "core"))
    place = jnp.stack([z, x, core]).astype(jnp.int32)

    own = over_x(
        call(
            pack_kernel,
            [((4, SEND_ROWS, LANES), bf16)],
            [
                ((length, features), bf16),
                ((2, head_count, length), f32),
                ((4, length, LANES), bf16),
                ((2, 1, length), jnp.int32),
                ((length, features), f32),
            ],
            layer_input[0],
            decay_first[0],
            decay_second[0],
            writes_first[0],
            reads_first[0],
            writes_second[0],
            reads_second[0],
            order_first.reshape(1, length),
            order_second.reshape(1, length),
            cotangent[0],
            scalars=0,
            anywhere=range(10),
            mib=60,
            copies=10,
            us=2,
        )
    )
    theirs = lax.dynamic_slice_in_dim(own, (1 - core) * PART_ROWS, PART_ROWS + SHARED_ROWS, axis=1)
    other = swap(theirs, "core")

    carry = ((2, LANES, LANES), f32)
    saved = ((BLOCKS, 2, 2 * LANES, LANES), bf16)
    half_grid = ((2, 512, LANES), bf16)
    block = ((BLOCKS, 2, BLOCK, LANES), bf16)
    grids = ((2, 2, 512, LANES), f32)
    few = ((8, LANES), f32)

    tok, cot, sh, end, rows, run = call(
        gather_kernel,
        [
            ((BLOCKS, TOKEN_ROWS, LANES), bf16),
            ((BLOCKS, COT_ROWS, LANES), bf16),
            ((BLOCKS, SHARED_ROWS, LANES), bf16),
            carry,
            ((2, BLOCKS, 32, LANES), bf16),
            ((BLOCKS, 8, LANES), f32),
        ],
        [carry, carry],
        place,
        own,
        other,
        anywhere=(1, 2),
        copies=24,
    )
    end = swap(end, "z")
    keep, send, states = call(
        first_forward,
        [half_grid, half_grid, saved],
        [carry],
        place,
        skip_first,
        rows,
        run,
        tok,
        sh,
        end,
        scalars=2,
    )
    got = swap(send, "z")
    keep_back, send_back, adjoints = call(
        first_backward,
        [half_grid, half_grid, saved],
        [carry],
        place,
        skip_second,
        rows,
        run,
        sh,
        cot,
        end,
        scalars=2,
    )
    got_back = swap(send_back, "z")
    u2, end, skip_two = call(
        regrid_forward, [block, carry, few], [grids], place, rows, sh, cot, keep, got
    )
    end = lax.ppermute(end, "z", [(0, 1)])
    dy1, end_own = call(
        regrid_backward,
        [block, ((2 * LANES + 8, LANES), f32)],
        [grids, few, carry],
        place,
        rows,
        tok,
        sh,
        keep_back,
        got_back,
        skip_two,
    )
    end_back = swap(end_own, "z")

    out_two = call(
        second_forward,
        [((2, 4, 272, LANES), bf16)],
        [carry],
        place,
        rows,
        run,
        sh,
        cot,
        u2,
        adjoints,
        end,
        us=8,
    )
    clips = lax.axis_size("dp")
    out, skip_sums = call(
        second_backward,
        [((2, 4, 528, LANES), bf16), ((clips, 8, LANES), f32)],
        [carry],
        place,
        skip_first,
        rows,
        run,
        tok,
        sh,
        dy1,
        states,
        end_back,
        end_own,
        out_two,
        scalars=2,
        anywhere=(10,),
        us=8,
    )
    skip_sums = lax.all_to_all(skip_sums, "dp", split_axis=0, concat_axis=0, tiled=True)
    back = over_x(
        call(
            pair_kernel,
            [((4, 1120, LANES), bf16)],
            [],
            out,
            swap(pick_slot(out), "core"),
            out_two,
            swap(pick_slot(out_two), "core"),
            skip_sums,
            swap(skip_sums, "core"),
            scalars=0,
            us=1,
        )
    )
    vector = ((length, LANES), bf16)
    decay = ((head_count, length), f32)
    skip = ((1, head_count), f32)
    grad_input, w1, r1, w2, r2, decay1, decay2, skip1, skip2 = call(
        last_kernel,
        [((length, features), bf16), vector, vector, vector, vector, decay, decay, skip, skip],
        [],
        place,
        back,
        us=1,
    )
    return (
        grad_input[None],
        w1[None],
        r1[None],
        decay1[None],
        skip1.reshape(head_count),
        w2[None],
        r2[None],
        decay2[None],
        skip2.reshape(head_count),
    )


def solution(mesh):
    finer = Mesh(mesh.devices.reshape(-1, 2, 4, 2), ("dp", "z", "x", "core"))
    seq = ("z", "x", "core")
    by_token, by_decay = P("dp", seq, None), P("dp", None, seq)
    return jax.shard_map(
        on_device,
        mesh=finer,
        in_specs=(
            by_token,
            by_token,
            by_token,
            by_decay,
            P(),
            by_token,
            by_token,
            by_decay,
            P(),
            P(seq),
            P(seq),
            by_token,
        ),
        out_specs=(
            by_token,
            by_token,
            by_token,
            by_decay,
            P(),
            by_token,
            by_token,
            by_decay,
            P(),
        ),
        check_vma=False,
    )
```

```python
import math

import jax
import jax.numpy as jnp
from jax import lax
from jax.experimental import pallas as pl
from jax.experimental.pallas import tpu as pltpu
from jax.sharding import Mesh
from jax.sharding import PartitionSpec as P

COLS = 32
ROWS = 64
BLOCK = 128
HALF = 64
LANES = 128
PART_ROWS = 784
TOKEN_ROWS = 272
SHARED_ROWS = 528
SEND_ROWS = 2 * PART_ROWS + SHARED_ROWS
COT_ROWS = 512
BLOCKS = 8
SKIP_SCALE = 1.0 / math.sqrt(16 * 2048 * 64)
UNROLL = {"gather": 8, "first": 4, "regrid": 8, "second": 4}

f32 = jnp.float32
bf16 = jnp.bfloat16


def nn(a, b):
    return lax.dot_general(a, b, (((1,), (0,)), ((), ())), preferred_element_type=f32)


def nt(a, b):
    return lax.dot_general(a, b, (((1,), (1,)), ((), ())), preferred_element_type=f32)


def tn(a, b):
    return lax.dot_general(a, b, (((0,), (0,)), ((), ())), preferred_element_type=f32)


def down(*values):
    return jnp.concatenate(values, axis=0)


def across(*values):
    return jnp.concatenate(values, axis=1)


def parts(values):
    hi = values.astype(bf16)
    return hi, (values - hi.astype(f32)).astype(bf16)


def iota(dim):
    return lax.broadcasted_iota(jnp.int32, (BLOCK, BLOCK), dim)


def one_where(cond):
    return jnp.where(cond, f32(1.0), f32(0.0))


def constants():
    row, col = iota(0), iota(1)
    lower = one_where(col <= row)
    before = one_where(row < col)
    head_a = one_where(col < HALF)
    head_b = 1.0 - head_a
    return {
        "head_a": head_a.astype(bf16),
        "head_b": head_b.astype(bf16),
        "causal": col <= row,
        "lower_bf": lower.astype(bf16),
        "grown": spread_matrix(12, 4, 2, HALF),
        "left": spread_matrix(20, 4, 2, HALF),
        "all": across(
            spread_matrix(0, 4, 3, LANES), spread_matrix(12, 4, 2, HALF), spread_matrix(20, 4, 2, HALF)
        ),
        "before": before,
        "sums": down(lower, before, jnp.ones((BLOCK, BLOCK), f32)).astype(bf16),
        "same": one_where(row == col),
        "mirror_row": one_where(row + col == 2 * (row - row % COLS) + COLS - 1),
        "mirror_col": one_where(row + col == 2 * (row - row % ROWS) + ROWS - 1),
    }


def decay_rows_of(tok_ref):
    small = down(*(tok_ref[b, 256:272, :] for b in range(BLOCKS)))
    row, col = iota(0), iota(1)
    sums = nn(small, one_where(row <= col).astype(bf16)).reshape(BLOCKS, 16, LANES)
    running = sums[:, 0:8] + sums[:, 8:16]
    hi = running.astype(bf16).astype(f32)
    mid = (running - hi).astype(bf16).astype(f32)
    grown = jnp.exp(running)
    left = jnp.exp(running[:, :, LANES - 1 :] - running)
    grown_hi, left_hi = grown.astype(bf16).astype(f32), left.astype(bf16).astype(f32)
    pieces = (hi, mid, running - hi - mid, grown_hi, grown - grown_hi, left_hi, left - left_hi)
    zeros = jnp.zeros((BLOCKS, 4, LANES), f32)
    layers = [
        jnp.concatenate([p[:, 4 * k : 4 * k + 4] for p in pieces] + [zeros], axis=1) for k in range(2)
    ]
    return running, [one.astype(bf16) for one in layers]


def spread_matrix(first, count, copies, width):
    row = lax.broadcasted_iota(jnp.int32, (32, count * width), 0)
    col = lax.broadcasted_iota(jnp.int32, (32, count * width), 1)
    inside = (row >= first) & (row < first + copies * count)
    return one_where(inside & ((row - first) % count == col // width)).astype(bf16)


def decay_scales(c, rows_ref, b, layer, which):
    rows = rows_ref[layer, b]
    values = tn(rows, c[which])
    if which == "grown":
        total = values[BLOCK - 1 :, :]
    else:
        total = tn(rows, c["grown"])[BLOCK - 1 :, :]
    return [(values[:, LANES * g : LANES * g + LANES], total[:, LANES * g : LANES * g + LANES]) for g in range(2)]


def decay_block(c, rows_ref, run_ref, b, layer):
    rows = rows_ref[layer, b]
    values = tn(rows, c["all"])
    running = run_ref[b]
    decays = [
        jnp.where(
            c["causal"],
            jnp.exp(
                jnp.minimum(
                    values[:, LANES * k : LANES * k + LANES] - running[4 * layer + k : 4 * layer + k + 1], 0.0
                )
            ),
            0.0,
        )
        for k in range(4)
    ]
    both = []
    for g in range(2):
        grown = values[:, 512 + LANES * g : 640 + LANES * g]
        left = values[:, 768 + LANES * g : 896 + LANES * g]
        both.append((decays[2 * g], decays[2 * g + 1], grown, left, grown[BLOCK - 1 :, :]))
    return both


def by_head(c, values):
    return down(values * c["head_a"], values * c["head_b"])


def mirror(c, sh_ref, b, layer):
    flags = sh_ref[b, 512:528, :].astype(f32)[layer : layer + 1]
    turned = c["mirror_col"] if layer else c["mirror_row"]
    return (flags * turned + (1.0 - flags) * c["same"]).astype(bf16)


def vectors(sh_ref, b, layer):
    at = 256 * layer
    return sh_ref[b, at : at + 128, :], sh_ref[b, at + 128 : at + 256, :]


def inputs_of(tok_ref, b, group):
    return tok_ref[b, 128 * group : 128 * group + 128, :]


def cotangent_of(cot_ref, b, group):
    at = 128 * group
    return cot_ref[b, at : at + 128, :], cot_ref[b, at + 256 : at + 384, :]


def skip_row(place_ref, skip_ref, group):
    at = 4 * (2 * place_ref[1] + place_ref[2]) + 2 * group
    lane = lax.broadcasted_iota(jnp.int32, (1, LANES), 1)
    return jnp.where(lane < HALF, skip_ref[at], skip_ref[at + 1])


def update(carry_ref, totals, vector, values):
    halves = [parts(v) if not isinstance(v, tuple) else v for v in values]
    moved = tn(vector, across(halves[0][0], halves[1][0], halves[0][1], halves[1][1]))
    for g in range(2):
        at = LANES * g
        carry_ref[g] = (
            totals[g] * carry_ref[g] + moved[:, at : at + LANES] + moved[:, 2 * LANES + at : 3 * LANES + at]
        )


def update_pair(scale, carry, vector, values):
    return scale * carry + tn(down(vector, vector), down(*parts(values)))


def load(pairs, sems):
    copies = [pltpu.make_async_copy(a, b, sems.at[i]) for i, (a, b) in enumerate(pairs)]
    for one in copies:
        one.start()
    for one in copies:
        one.wait()


def over_blocks(step, kind):
    lax.fori_loop(0, BLOCKS, lambda i, _: step(i), None, unroll=UNROLL[kind])


def pack_kernel(
    u_any, d1_any, d2_any, w1, r1, w2, r2, o1_any, o2_any, cot_any, out_ref, u_ref, d_ref, v_ref, o_ref, cot_ref, sems
):
    load(
        [(cot_any, cot_ref), (u_any, u_ref), (d1_any, d_ref.at[0]), (d2_any, d_ref.at[1])]
        + [(ref, v_ref.at[k]) for k, ref in enumerate((w1, r1, w2, r2))]
        + [(o1_any, o_ref.at[0]), (o2_any, o_ref.at[1])],
        sems,
    )
    lane = lax.broadcasted_iota(jnp.int32, (1, LANES), 1)
    row_flip = one_where(jnp.bitwise_and(o_ref[0], COLS - 1) != jnp.bitwise_and(lane, COLS - 1))
    col_flip = one_where(
        lax.shift_right_logical(o_ref[1], COLS.bit_length() - 1) != jnp.bitwise_and(lane, ROWS - 1)
    )
    flags = down(row_flip, col_flip, jnp.zeros((14, LANES), f32)).astype(bf16)
    for dest in range(8):
        x, core = dest // 2, dest % 2
        at = core * (PART_ROWS + SHARED_ROWS)
        for group in range(2):
            lanes = slice((2 * dest + group) * LANES, (2 * dest + group + 1) * LANES)
            row = at + 128 * group
            out_ref[x, row : row + 128, :] = u_ref[:, lanes]
            hi, lo = parts(cot_ref[:, lanes])
            row += TOKEN_ROWS
            out_ref[x, row : row + 128, :] = hi
            out_ref[x, row + 256 : row + 384, :] = lo
        decays = down(*(d_ref[layer, 4 * dest : 4 * dest + 4, :] for layer in range(2)))
        hi, lo = parts(decays)
        out_ref[x, at + 256 : at + 272, :] = down(hi.astype(f32), lo.astype(f32)).astype(bf16)
    for x in range(4):
        for k in range(4):
            at = PART_ROWS + 128 * k
            out_ref[x, at : at + 128, :] = v_ref[k]
        out_ref[x, PART_ROWS + 512 : PART_ROWS + 528, :] = flags


def gather_kernel(
    place_ref, own, other, tok_ref, cot_ref, sh_ref, ends_ref, rows_ref, run_ref, s_ref, a_ref, sems
):
    z, core = place_ref[0], place_ref[2]
    mine = pl.multiple_of(core * (PART_ROWS + SHARED_ROWS), 16)
    part = pl.multiple_of(core * SHARED_ROWS, 16)
    share = pl.multiple_of((1 - core) * PART_ROWS, 16)
    tokens, vectors_in, cotangents = [], [], []
    for x in range(4):
        near, far = 2 * x + core, 2 * x + 1 - core
        tokens += [
            (own.at[x, pl.ds(mine, TOKEN_ROWS)], tok_ref.at[near]),
            (other.at[x, pl.ds(part, TOKEN_ROWS)], tok_ref.at[far]),
        ]
        vectors_in += [
            (own.at[x, pl.ds(PART_ROWS, SHARED_ROWS)], sh_ref.at[near]),
            (other.at[x, pl.ds(share, SHARED_ROWS)], sh_ref.at[far]),
        ]
        cotangents += [
            (own.at[x, pl.ds(mine + TOKEN_ROWS, COT_ROWS)], cot_ref.at[near]),
            (other.at[x, pl.ds(part + TOKEN_ROWS, COT_ROWS)], cot_ref.at[far]),
        ]
    copies = [
        pltpu.make_async_copy(a, b, sems.at[i])
        for i, (a, b) in enumerate(tokens + vectors_in + cotangents)
    ]
    for one in copies:
        one.start()
    c = constants()
    s_ref[...] = jnp.zeros_like(s_ref)
    a_ref[...] = jnp.zeros_like(a_ref)
    for one in copies[:8]:
        one.wait()
    running, layers = decay_rows_of(tok_ref)
    run_ref[...] = running
    for k in range(2):
        rows_ref[k] = layers[k]
    for one in copies[8:16]:
        one.wait()

    def forward(b):
        writes, _ = vectors(sh_ref, b, 0)
        scale = decay_scales(c, rows_ref, b, 0, "left")
        values = [inputs_of(tok_ref, b, g).astype(f32) * scale[g][0] for g in range(2)]
        update(s_ref, [one[1] for one in scale], writes, values)

    def backward(i):
        b = BLOCKS - 1 - i
        _, reads = vectors(sh_ref, b, 1)
        scale = decay_scales(c, rows_ref, b, 1, "grown")
        values = []
        for group in range(2):
            hi, lo = cotangent_of(cot_ref, b, group)
            values.append((hi.astype(f32) + lo.astype(f32)) * scale[group][0])
        update(a_ref, [one[1] for one in scale], reads, values)

    over_blocks(forward, "gather")
    for one in copies[16:]:
        one.wait()
    over_blocks(backward, "gather")
    ends_ref[...] = jnp.where(z == 0, s_ref[...], a_ref[...]).astype(bf16)


def pick_second(source, out_ref, sems):
    load([(source.at[1, x], out_ref.at[x]) for x in range(4)], sems)


def first_forward(place_ref, skip_ref, rows_ref, run_ref, tok_ref, sh_ref, ends_ref, keep_ref, send_ref, state_ref, s_ref):
    z = place_ref[0]
    c = constants()
    s_ref[...] = jnp.where(z == 1, ends_ref[...].astype(f32), 0.0)

    def step(b):
        writes, reads = vectors(sh_ref, b, 0)
        scores = nt(reads, writes)
        turn = mirror(c, sh_ref, b, 0)
        for group, (decay_a, decay_b, grown, left, total) in enumerate(
            decay_block(c, rows_ref, run_ref, b, 0)
        ):
            u = inputs_of(tok_ref, b, group)
            mixed = across(*parts(across(decay_a * scores, decay_b * scores)))
            state = s_ref[group]
            state_both = down(*parts(state))
            state_ref[b, group] = state_both
            u32 = u.astype(f32)
            heads = by_head(c, u)
            y = (
                nn(mixed, down(heads, heads))
                + grown * nn(across(reads, reads), state_both)
                + skip_row(place_ref, skip_ref, group) * u32
            )
            s_ref[group] = update_pair(total, state, writes, u32 * left)
            grid = nn(turn, y.astype(bf16)).astype(bf16)
            for k in range(4):
                near, far = grid[32 * k : 32 * k + 16], grid[32 * k + 16 : 32 * k + 32]
                at = pl.multiple_of(64 * b + 16 * k, 16)
                keep_ref[group, pl.ds(at, 16), :] = jnp.where(z == 0, near, far)
                send_ref[group, pl.ds(at, 16), :] = jnp.where(z == 0, far, near)

    over_blocks(step, "first")


def first_backward(place_ref, skip_ref, rows_ref, run_ref, sh_ref, cot_ref, ends_ref, keep_ref, send_ref, adjoint_ref, a_ref):
    z = place_ref[0]
    c = constants()
    a_ref[...] = jnp.where(z == 0, ends_ref[...].astype(f32), 0.0)

    def step(i):
        b = BLOCKS - 1 - i
        writes, reads = vectors(sh_ref, b, 1)
        scores = nt(reads, writes)
        turn = mirror(c, sh_ref, b, 1)
        for group, (decay_a, decay_b, grown, left, total) in enumerate(
            decay_block(c, rows_ref, run_ref, b, 1)
        ):
            hi, lo = cotangent_of(cot_ref, b, group)
            mixed, mixed_low = parts(down(decay_a * scores, decay_b * scores))
            adjoint = a_ref[group]
            adjoint_both = down(*parts(adjoint))
            adjoint_ref[b, group] = adjoint_both
            dy = hi.astype(f32) + lo.astype(f32)
            hi_heads, lo_heads = by_head(c, hi), by_head(c, lo)
            du = (
                tn(down(mixed, mixed_low, mixed), down(hi_heads, hi_heads, lo_heads))
                + left * nn(across(writes, writes), adjoint_both)
                + skip_row(place_ref, skip_ref, group) * dy
            )
            a_ref[group] = update_pair(total, adjoint, reads, dy * grown)
            grid = nn(turn, du.astype(bf16)).astype(bf16)
            for k in range(2):
                near, far = grid[64 * k : 64 * k + 32], grid[64 * k + 32 : 64 * k + 64]
                at = pl.multiple_of(64 * b + 32 * k, 32)
                keep_ref[group, pl.ds(at, 32), :] = jnp.where(z == 0, near, far)
                send_ref[group, pl.ds(at, 32), :] = jnp.where(z == 0, far, near)

    over_blocks(step, "first")


def regrid_forward(
    place_ref, rows_ref, sh_ref, cot_ref, keep_ref, got_ref, u2_ref, ends_ref, skip_ref, grid_ref, s_ref
):
    z = place_ref[0]
    c = constants()
    grid_ref[z] = keep_ref[...].astype(f32)
    grid_ref[1 - z] = got_ref[...].astype(f32)
    s_ref[...] = jnp.zeros_like(s_ref)
    skip_ref[...] = jnp.zeros_like(skip_ref)

    def step(b):
        writes, _ = vectors(sh_ref, b, 1)
        turn = mirror(c, sh_ref, b, 1)
        scale = decay_scales(c, rows_ref, b, 1, "left")
        values = []
        for group in range(2):
            picked = down(
                *(
                    grid_ref[part, group, pl.ds(2 * b + k, 32, stride=16), :]
                    for k in range(2)
                    for part in range(2)
                )
            )
            u32 = nn(turn, picked.astype(bf16))
            u2_ref[b, group] = u32.astype(bf16)
            values.append(u32 * scale[group][0])
            hi, lo = cotangent_of(cot_ref, b, group)
            dy = hi.astype(f32) + lo.astype(f32)
            skip_ref[group : group + 1, :] += jnp.sum(u32 * dy, axis=0, keepdims=True)
        update(s_ref, [one[1] for one in scale], writes, values)

    over_blocks(step, "regrid")
    ends_ref[...] = s_ref[...].astype(bf16)


def regrid_backward(
    place_ref, rows_ref, tok_ref, sh_ref, keep_ref, got_ref, skip_two_ref, dy1_ref, ends_ref, grid_ref, skip_ref, a_ref
):
    z = place_ref[0]
    c = constants()
    grid_ref[z] = keep_ref[...].astype(f32)
    grid_ref[1 - z] = got_ref[...].astype(f32)
    a_ref[...] = jnp.zeros_like(a_ref)
    skip_ref[0:2, :] = jnp.zeros((2, LANES), f32)
    skip_ref[2:8, :] = skip_two_ref[0:6, :]

    def step(i):
        b = BLOCKS - 1 - i
        _, reads = vectors(sh_ref, b, 0)
        turn = mirror(c, sh_ref, b, 0)
        scale = decay_scales(c, rows_ref, b, 0, "grown")
        values = []
        for group in range(2):
            picked = down(
                *(
                    grid_ref[part, group, pl.ds(4 * b + k, 16, stride=32), :]
                    for k in range(4)
                    for part in range(2)
                )
            )
            dy = nn(turn, picked.astype(bf16))
            dy1_ref[b, group] = dy.astype(bf16)
            values.append(dy * scale[group][0])
            u = inputs_of(tok_ref, b, group).astype(f32)
            skip_ref[group : group + 1, :] += jnp.sum(u * dy, axis=0, keepdims=True)
        update(a_ref, [one[1] for one in scale], reads, values)

    over_blocks(step, "regrid")
    for group in range(2):
        ends_ref[LANES * group : LANES * (group + 1), :] = a_ref[group]
    ends_ref[2 * LANES :, :] = skip_ref[...]


def block_gradients(c, rows_ref, run_ref, sh_ref, b, layer, u_of, dy_of, state_of, adjoint_of):
    writes, reads = vectors(sh_ref, b, layer)
    reads_two, writes_two = down(reads, reads), down(writes, writes)
    scores = nt(reads, writes)
    d_scores, d_writes, d_reads = 0.0, 0.0, 0.0
    decay_rows, kept = [], []
    for group, (decay_a, decay_b, grown, left, total) in enumerate(
        decay_block(c, rows_ref, run_ref, b, layer)
    ):
        u, (dy, dy_low) = u_of(group), dy_of(group)
        u32, dy32 = u.astype(f32), dy.astype(f32)
        dy_heads = by_head(c, dy)
        if dy_low is None:
            pairs = nt(dy_heads, u)
        else:
            pairs = nt(across(dy_heads, by_head(c, dy_low)), across(u, u))
            dy32 = dy32 + dy_low.astype(f32)
        pair_a, pair_b = decay_a * pairs[:BLOCK], decay_b * pairs[BLOCK:]
        d_scores = d_scores + pair_a + pair_b
        u_left, dy_grown = u32 * left, dy32 * grown
        u_hi, u_lo = parts(u_left)
        dy_hi, dy_lo = parts(dy_grown)
        state, adjoint = state_of(group), adjoint_of(group)
        read_state = nn(across(reads, reads), state)
        write_adjoint = nn(across(writes, writes), adjoint)
        state_hi, adjoint_hi = state[:LANES], adjoint[:LANES]
        d_writes = (
            d_writes
            + nt(across(u_hi, u_lo), across(adjoint_hi, adjoint_hi))
        )
        d_reads = (
            d_reads
            + nt(across(dy_hi, dy_lo), across(state_hi, state_hi))
        )
        crossing = across((pair_a * scores).astype(bf16), (pair_b * scores).astype(bf16))
        inner = tn(crossing, c["lower_bf"])
        products = down(
            (dy_grown * read_state).astype(bf16),
            (u_left * write_adjoint).astype(bf16),
            (total * (state_hi.astype(f32) * adjoint_hi.astype(f32))).astype(bf16),
        )
        outer = tn(products, c["sums"])
        for k in range(2):
            decay_rows.append(
                jnp.sum(c["before"] * inner[BLOCK * k : BLOCK * (k + 1)], axis=0, keepdims=True)
                + jnp.sum(outer[HALF * k : HALF * (k + 1)], axis=0, keepdims=True)
            )
        kept.append(
            {
                "total": total,
                "left": left,
                "u_left": down(u_hi, u_lo),
                "dy_grown": down(dy_hi, dy_lo),
                "write_adjoint": write_adjoint,
                "dy_heads": dy_heads,
                "dy": dy32,
                "mixed": lambda a=decay_a, h=decay_b: down(
                    (a * scores).astype(bf16), (h * scores).astype(bf16)
                ),
            }
        )
    low = parts(d_scores)
    d_writes = d_writes + tn(down(*low), reads_two)
    d_reads = d_reads + nn(across(*low), writes_two)
    return d_writes, d_reads, down(*decay_rows), kept, writes_two, reads_two


def put_gradients(out_ref, core, b, at, d_writes, d_reads, rows):
    slot, x = jnp.bitwise_xor(b % 2, core), b // 2
    out_ref[slot, x, at : at + 128, :] = d_writes.astype(bf16)
    out_ref[slot, x, at + 128 : at + 256, :] = d_reads.astype(bf16)
    hi, lo = parts(rows)
    small = down(hi.astype(f32), lo.astype(f32), jnp.zeros((8, LANES), f32))
    out_ref[slot, x, at + 256 : at + 272, :] = small.astype(bf16)


def second_forward(place_ref, rows_ref, run_ref, sh_ref, cot_ref, u2_ref, adjoint_ref, ends_ref, out_ref, s_ref):
    core = place_ref[2]
    c = constants()
    s_ref[...] = ends_ref[...].astype(f32)

    def step(b):
        d_writes, d_reads, rows, kept, writes_two, _ = block_gradients(
            c,
            rows_ref,
            run_ref,
            sh_ref,
            b,
            1,
            lambda g: u2_ref[b, g],
            lambda g: cotangent_of(cot_ref, b, g),
            lambda g: down(*parts(s_ref[g])),
            lambda g: adjoint_ref[b, g],
        )
        put_gradients(out_ref, core, b, 0, d_writes, d_reads, rows)
        for group in range(2):
            k = kept[group]
            s_ref[group] = k["total"] * s_ref[group] + tn(writes_two, k["u_left"])

    over_blocks(step, "second")


def second_backward(
    place_ref, skip_ref, rows_ref, run_ref, tok_ref, sh_ref, dy1_ref, state_ref, ends_ref, own_ref, _second, out_ref, sums_ref, a_ref
):
    core = place_ref[2]
    c = constants()
    for group in range(2):
        arrived = ends_ref[LANES * group : LANES * (group + 1), :]
        a_ref[group] = jnp.where(place_ref[0] == 0, arrived, 0.0)
    total = own_ref[2 * LANES :, :] + ends_ref[2 * LANES :, :]
    for k in range(sums_ref.shape[0]):
        sums_ref[k] = total

    def step(i):
        b = BLOCKS - 1 - i
        d_writes, d_reads, rows, kept, _, reads_two = block_gradients(
            c,
            rows_ref,
            run_ref,
            sh_ref,
            b,
            0,
            lambda g: inputs_of(tok_ref, b, g),
            lambda g: (dy1_ref[b, g], None),
            lambda g: state_ref[b, g],
            lambda g: down(*parts(a_ref[g])),
        )
        put_gradients(out_ref, core, b, 256, d_writes, d_reads, rows)
        slot = jnp.bitwise_xor(b % 2, core)
        for group in range(2):
            k = kept[group]
            du = (
                tn(k["mixed"](), k["dy_heads"])
                + k["left"] * k["write_adjoint"]
                + skip_row(place_ref, skip_ref, group) * k["dy"]
            )
            out_ref[slot, b // 2, 128 * group : 128 * group + 128, :] = du.astype(bf16)
            a_ref[group] = k["total"] * a_ref[group] + tn(reads_two, k["dy_grown"])

    over_blocks(step, "second")


def pair_kernel(own_ref, other_ref, own_two_ref, other_two_ref, skip_ref, skip_other_ref, out_ref):
    skips = []
    for ref in (skip_ref, skip_other_ref):
        total = ref[0, 0:4, :]
        for k in range(1, ref.shape[0]):
            total = total + ref[k, 0:4, :]
        hi = total.astype(bf16).astype(f32)
        mid, low = parts(total - hi)
        skips.append(down(hi, mid.astype(f32), low.astype(f32), jnp.zeros((4, LANES), f32)))
    skips = down(*skips).astype(bf16)
    for x in range(4):
        out_ref[x, 0:256, :] = own_ref[0, x, 0:256, :]
        out_ref[x, 256:512, :] = other_ref[x, 0:256, :]
        out_ref[x, 512:768, :] = (
            own_ref[0, x, 256:512, :].astype(f32) + other_ref[x, 256:512, :].astype(f32)
        ).astype(bf16)
        out_ref[x, 768:784, :] = own_ref[0, x, 512:528, :]
        out_ref[x, 784:800, :] = other_ref[x, 512:528, :]
        out_ref[x, 800:832, :] = skips
        out_ref[x, 832:1088, :] = (
            own_two_ref[0, x, 0:256, :].astype(f32) + other_two_ref[x, 0:256, :].astype(f32)
        ).astype(bf16)
        out_ref[x, 1088:1104, :] = own_two_ref[0, x, 256:272, :]
        out_ref[x, 1104:1120, :] = other_two_ref[x, 256:272, :]


def last_kernel(place_ref, back_ref, grad_ref, w1, r1, w2, r2, decay1_ref, decay2_ref, skip1_ref, skip2_ref):
    core = place_ref[2]

    def chosen(ref, x, at, size, owner):
        near, far = ref[x, at : at + size, :], ref[x, at + size : at + 2 * size, :]
        return jnp.where(core == owner, near, far)

    lanes = []
    for x in range(4):
        for owner in range(2):
            both = chosen(back_ref, x, 0, 256, owner)
            for group in range(2):
                at = ((2 * x + owner) * 2 + group) * LANES
                grad_ref[:, at : at + LANES] = both[128 * group : 128 * group + 128]
            at = (2 * x + owner) * 4
            small = chosen(back_ref, x, 768, 16, owner).astype(f32)
            decay1_ref[at : at + 4, :] = small[0:4] + small[4:8]
            small = chosen(back_ref, x, 1088, 16, owner).astype(f32)
            decay2_ref[at : at + 4, :] = small[0:4] + small[4:8]
            small = chosen(back_ref, x, 800, 16, owner).astype(f32)
            lanes.append(small[0:4] + small[4:8] + small[8:12])
    lanes = down(*lanes)
    row, head = (lax.broadcasted_iota(jnp.int32, (32, 32), k) for k in range(2))
    lane, side = (lax.broadcasted_iota(jnp.int32, (LANES, 32), k) for k in range(2))
    folded = lax.dot_general(
        lanes,
        one_where(lane // HALF == side % 2),
        (((1,), (0,)), ((), ())),
        precision=lax.Precision.HIGHEST,
        preferred_element_type=f32,
    )
    owner = (row // 4 == head // 4) & (row % 2 == head // 2 % 2)
    for layer, ref in enumerate((skip1_ref, skip2_ref)):
        kept = jnp.where(owner & (row // 2 % 2 == layer), folded, 0.0)
        ref[...] = jnp.sum(kept, axis=0, keepdims=True) * SKIP_SCALE
    for ref, at in ((w1, 512), (r1, 640), (w2, 832), (r2, 960)):
        total = back_ref[0, at : at + 128, :].astype(f32)
        for x in range(1, 4):
            total = total + back_ref[x, at : at + 128, :].astype(f32)
        ref[...] = total.astype(bf16)


def call(kernel, outs, scratch, *args, scalars=1, anywhere=(), copies=0, us=5, mib=12):
    shapes = [jax.ShapeDtypeStruct(s, d) for s, d in outs]
    many = len(shapes) > 1
    in_specs = [
        pl.BlockSpec(
            memory_space=pltpu.SMEM if i < scalars else pl.ANY if i in anywhere else pltpu.VMEM
        )
        for i in range(len(args))
    ]
    out_specs = [pl.BlockSpec(memory_space=pltpu.VMEM)] * len(shapes)
    scratch = [pltpu.VMEM(s, d) for s, d in scratch]
    if copies:
        scratch.append(pltpu.SemaphoreType.DMA((copies,)))
    return pl.pallas_call(
        kernel,
        out_shape=shapes if many else shapes[0],
        in_specs=in_specs,
        out_specs=out_specs if many else out_specs[0],
        scratch_shapes=scratch,
        cost_estimate=pl.CostEstimate(flops=us * 10**9, bytes_accessed=10**6, transcendentals=0),
        compiler_params=pltpu.CompilerParams(vmem_limit_bytes=mib * 2**20),
        name=kernel.__name__,
    )(*args)


def pick_slot(values):
    out = (values.shape[1:], bf16)
    return call(pick_second, [out], [], values, scalars=0, anywhere=(0,), copies=4, us=1)


def swap(values, axis):
    return lax.ppermute(values, axis, [(0, 1), (1, 0)])


def over_x(values):
    return lax.all_to_all(values, "x", split_axis=0, concat_axis=0, tiled=True)


def on_device(
    layer_input,
    writes_first,
    reads_first,
    decay_first,
    skip_first,
    writes_second,
    reads_second,
    decay_second,
    skip_second,
    order_first,
    order_second,
    cotangent,
):
    length, features = layer_input.shape[1:]
    head_count = skip_first.shape[0]
    head_size = features // head_count
    z, x, core = (lax.axis_index(a) for a in ("z", "x", "core"))
    place = jnp.stack([z, x, core]).astype(jnp.int32)

    own = over_x(
        call(
            pack_kernel,
            [((4, SEND_ROWS, LANES), bf16)],
            [
                ((length, features), bf16),
                ((2, head_count, length), f32),
                ((4, length, LANES), bf16),
                ((2, 1, length), jnp.int32),
                ((length, features), f32),
            ],
            layer_input[0],
            decay_first[0],
            decay_second[0],
            writes_first[0],
            reads_first[0],
            writes_second[0],
            reads_second[0],
            order_first.reshape(1, length),
            order_second.reshape(1, length),
            cotangent[0],
            scalars=0,
            anywhere=range(10),
            mib=60,
            copies=10,
            us=2,
        )
    )
    theirs = lax.dynamic_slice_in_dim(own, (1 - core) * PART_ROWS, PART_ROWS + SHARED_ROWS, axis=1)
    other = swap(theirs, "core")

    carry = ((2, LANES, LANES), f32)
    sent = ((2, LANES, LANES), bf16)
    saved = ((BLOCKS, 2, 2 * LANES, LANES), bf16)
    half_grid = ((2, 512, LANES), bf16)
    block = ((BLOCKS, 2, BLOCK, LANES), bf16)
    grids = ((2, 2, 512, LANES), f32)
    few = ((8, LANES), f32)

    tok, cot, sh, end, rows, run = call(
        gather_kernel,
        [
            ((BLOCKS, TOKEN_ROWS, LANES), bf16),
            ((BLOCKS, COT_ROWS, LANES), bf16),
            ((BLOCKS, SHARED_ROWS, LANES), bf16),
            sent,
            ((2, BLOCKS, 32, LANES), bf16),
            ((BLOCKS, 8, LANES), f32),
        ],
        [carry, carry],
        place,
        own,
        other,
        anywhere=(1, 2),
        copies=24,
    )
    end = swap(end, "z")
    keep, send, states = call(
        first_forward,
        [half_grid, half_grid, saved],
        [carry],
        place,
        skip_first,
        rows,
        run,
        tok,
        sh,
        end,
        scalars=2,
    )
    got = swap(send, "z")
    keep_back, send_back, adjoints = call(
        first_backward,
        [half_grid, half_grid, saved],
        [carry],
        place,
        skip_second,
        rows,
        run,
        sh,
        cot,
        end,
        scalars=2,
    )
    got_back = swap(send_back, "z")
    u2, end, skip_two = call(
        regrid_forward, [block, sent, few], [grids, carry], place, rows, sh, cot, keep, got
    )
    end = lax.ppermute(end, "z", [(0, 1)])
    dy1, end_own = call(
        regrid_backward,
        [block, ((2 * LANES + 8, LANES), f32)],
        [grids, few, carry],
        place,
        rows,
        tok,
        sh,
        keep_back,
        got_back,
        skip_two,
    )
    end_back = swap(end_own, "z")

    out_two = call(
        second_forward,
        [((2, 4, 272, LANES), bf16)],
        [carry],
        place,
        rows,
        run,
        sh,
        cot,
        u2,
        adjoints,
        end,
        us=8,
    )
    clips = lax.axis_size("dp")
    out, skip_sums = call(
        second_backward,
        [((2, 4, 528, LANES), bf16), ((clips, 8, LANES), f32)],
        [carry],
        place,
        skip_first,
        rows,
        run,
        tok,
        sh,
        dy1,
        states,
        end_back,
        end_own,
        out_two,
        scalars=2,
        anywhere=(10,),
        us=8,
    )
    skip_sums = lax.all_to_all(skip_sums, "dp", split_axis=0, concat_axis=0, tiled=True)
    back = over_x(
        call(
            pair_kernel,
            [((4, 1120, LANES), bf16)],
            [],
            out,
            swap(pick_slot(out), "core"),
            out_two,
            swap(pick_slot(out_two), "core"),
            skip_sums,
            swap(skip_sums, "core"),
            scalars=0,
            us=1,
        )
    )
    vector = ((length, LANES), bf16)
    decay = ((head_count, length), f32)
    skip = ((1, head_count), f32)
    grad_input, w1, r1, w2, r2, decay1, decay2, skip1, skip2 = call(
        last_kernel,
        [((length, features), bf16), vector, vector, vector, vector, decay, decay, skip, skip],
        [],
        place,
        back,
        us=1,
    )
    return (
        grad_input[None],
        w1[None],
        r1[None],
        decay1[None],
        skip1.reshape(head_count),
        w2[None],
        r2[None],
        decay2[None],
        skip2.reshape(head_count),
    )


def solution(mesh):
    finer = Mesh(mesh.devices.reshape(-1, 2, 4, 2), ("dp", "z", "x", "core"))
    seq = ("z", "x", "core")
    by_token, by_decay = P("dp", seq, None), P("dp", None, seq)
    return jax.shard_map(
        on_device,
        mesh=finer,
        in_specs=(
            by_token,
            by_token,
            by_token,
            by_decay,
            P(),
            by_token,
            by_token,
            by_decay,
            P(),
            P(seq),
            P(seq),
            by_token,
        ),
        out_specs=(
            by_token,
            by_token,
            by_token,
            by_decay,
            P(),
            by_token,
            by_token,
            by_decay,
            P(),
        ),
        check_vma=False,
    )
```

```python
import math

import jax
import jax.numpy as jnp
from jax import lax
from jax.experimental import pallas as pl
from jax.experimental.pallas import tpu as pltpu
from jax.sharding import Mesh
from jax.sharding import PartitionSpec as P

COLS = 32
ROWS = 64
BLOCK = 128
HALF = 64
LANES = 128
PART_ROWS = 784
TOKEN_ROWS = 272
SHARED_ROWS = 528
SEND_ROWS = 2 * PART_ROWS + SHARED_ROWS
COT_ROWS = 512
BLOCKS = 8
SKIP_SCALE = 1.0 / math.sqrt(16 * 2048 * 64)
UNROLL = {"gather": 8, "first": 8, "regrid": 8, "second": 8}

f32 = jnp.float32
bf16 = jnp.bfloat16


def nn(a, b):
    return lax.dot_general(a, b, (((1,), (0,)), ((), ())), preferred_element_type=f32)


def nt(a, b):
    return lax.dot_general(a, b, (((1,), (1,)), ((), ())), preferred_element_type=f32)


def tn(a, b):
    return lax.dot_general(a, b, (((0,), (0,)), ((), ())), preferred_element_type=f32)


def down(*values):
    return jnp.concatenate(values, axis=0)


def across(*values):
    return jnp.concatenate(values, axis=1)


def parts(values):
    hi = values.astype(bf16)
    return hi, (values - hi.astype(f32)).astype(bf16)


def iota(dim):
    return lax.broadcasted_iota(jnp.int32, (BLOCK, BLOCK), dim)


def one_where(cond):
    return jnp.where(cond, f32(1.0), f32(0.0))


def constants():
    row, col = iota(0), iota(1)
    lower = one_where(col <= row)
    before = one_where(row < col)
    head_a = one_where(col < HALF)
    head_b = 1.0 - head_a
    return {
        "head_a": head_a.astype(bf16),
        "head_b": head_b.astype(bf16),
        "causal": col <= row,
        "lower_bf": lower.astype(bf16),
        "grown": spread_matrix(12, 4, 2, HALF),
        "left": spread_matrix(20, 4, 2, HALF),
        "all": across(
            spread_matrix(0, 4, 3, LANES), spread_matrix(12, 4, 2, HALF), spread_matrix(20, 4, 2, HALF)
        ),
        "before": before,
        "sums": down(lower, before, jnp.ones((BLOCK, BLOCK), f32)).astype(bf16),
        "same": one_where(row == col),
        "mirror_row": one_where(row + col == 2 * (row - row % COLS) + COLS - 1),
        "mirror_col": one_where(row + col == 2 * (row - row % ROWS) + ROWS - 1),
    }


def decay_rows_of(tok_ref):
    small = down(*(tok_ref[b, 256:272, :] for b in range(BLOCKS)))
    row, col = iota(0), iota(1)
    sums = nn(small, one_where(row <= col).astype(bf16)).reshape(BLOCKS, 16, LANES)
    running = sums[:, 0:8] + sums[:, 8:16]
    hi = running.astype(bf16).astype(f32)
    mid = (running - hi).astype(bf16).astype(f32)
    grown = jnp.exp(running)
    left = jnp.exp(running[:, :, LANES - 1 :] - running)
    grown_hi, left_hi = grown.astype(bf16).astype(f32), left.astype(bf16).astype(f32)
    pieces = (hi, mid, running - hi - mid, grown_hi, grown - grown_hi, left_hi, left - left_hi)
    zeros = jnp.zeros((BLOCKS, 4, LANES), f32)
    layers = [
        jnp.concatenate([p[:, 4 * k : 4 * k + 4] for p in pieces] + [zeros], axis=1) for k in range(2)
    ]
    return running, [one.astype(bf16) for one in layers]


def spread_matrix(first, count, copies, width):
    row = lax.broadcasted_iota(jnp.int32, (32, count * width), 0)
    col = lax.broadcasted_iota(jnp.int32, (32, count * width), 1)
    inside = (row >= first) & (row < first + copies * count)
    return one_where(inside & ((row - first) % count == col // width)).astype(bf16)


def decay_scales(c, rows_ref, b, layer, which):
    rows = rows_ref[layer, b]
    values = tn(rows, c[which])
    if which == "grown":
        total = values[BLOCK - 1 :, :]
    else:
        total = tn(rows, c["grown"])[BLOCK - 1 :, :]
    return [(values[:, LANES * g : LANES * g + LANES], total[:, LANES * g : LANES * g + LANES]) for g in range(2)]


def decay_block(c, rows_ref, run_ref, b, layer):
    rows = rows_ref[layer, b]
    values = tn(rows, c["all"])
    running = run_ref[b]
    decays = [
        jnp.where(
            c["causal"],
            jnp.exp(
                jnp.minimum(
                    values[:, LANES * k : LANES * k + LANES] - running[4 * layer + k : 4 * layer + k + 1], 0.0
                )
            ),
            0.0,
        )
        for k in range(4)
    ]
    both = []
    for g in range(2):
        grown = values[:, 512 + LANES * g : 640 + LANES * g]
        left = values[:, 768 + LANES * g : 896 + LANES * g]
        both.append((decays[2 * g], decays[2 * g + 1], grown, left, grown[BLOCK - 1 :, :]))
    return both


def by_head(c, values):
    return down(values * c["head_a"], values * c["head_b"])


def mirror(c, sh_ref, b, layer):
    flags = sh_ref[b, 512:528, :].astype(f32)[layer : layer + 1]
    turned = c["mirror_col"] if layer else c["mirror_row"]
    return (flags * turned + (1.0 - flags) * c["same"]).astype(bf16)


def vectors(sh_ref, b, layer):
    at = 256 * layer
    return sh_ref[b, at : at + 128, :], sh_ref[b, at + 128 : at + 256, :]


def inputs_of(tok_ref, b, group):
    return tok_ref[b, 128 * group : 128 * group + 128, :]


def cotangent_of(cot_ref, b, group):
    at = 128 * group
    return cot_ref[b, at : at + 128, :], cot_ref[b, at + 256 : at + 384, :]


def skip_row(place_ref, skip_ref, group):
    at = 4 * (2 * place_ref[1] + place_ref[2]) + 2 * group
    lane = lax.broadcasted_iota(jnp.int32, (1, LANES), 1)
    return jnp.where(lane < HALF, skip_ref[at], skip_ref[at + 1])


def update(carry_ref, totals, vector, values):
    halves = [parts(v) if not isinstance(v, tuple) else v for v in values]
    moved = tn(vector, across(halves[0][0], halves[1][0], halves[0][1], halves[1][1]))
    for g in range(2):
        at = LANES * g
        carry_ref[g] = (
            totals[g] * carry_ref[g] + moved[:, at : at + LANES] + moved[:, 2 * LANES + at : 3 * LANES + at]
        )


def update_pair(scale, carry, vector, values):
    return scale * carry + tn(down(vector, vector), down(*parts(values)))


def load(pairs, sems):
    copies = [pltpu.make_async_copy(a, b, sems.at[i]) for i, (a, b) in enumerate(pairs)]
    for one in copies:
        one.start()
    for one in copies:
        one.wait()


def over_blocks(step, kind):
    lax.fori_loop(0, BLOCKS, lambda i, _: step(i), None, unroll=UNROLL[kind])


def pack_kernel(
    u_any, d1_any, d2_any, w1, r1, w2, r2, o1_any, o2_any, cot_any, out_ref, u_ref, d_ref, v_ref, o_ref, cot_ref, sems
):
    load(
        [(cot_any, cot_ref), (u_any, u_ref), (d1_any, d_ref.at[0]), (d2_any, d_ref.at[1])]
        + [(ref, v_ref.at[k]) for k, ref in enumerate((w1, r1, w2, r2))]
        + [(o1_any, o_ref.at[0]), (o2_any, o_ref.at[1])],
        sems,
    )
    lane = lax.broadcasted_iota(jnp.int32, (1, LANES), 1)
    row_flip = one_where(jnp.bitwise_and(o_ref[0], COLS - 1) != jnp.bitwise_and(lane, COLS - 1))
    col_flip = one_where(
        lax.shift_right_logical(o_ref[1], COLS.bit_length() - 1) != jnp.bitwise_and(lane, ROWS - 1)
    )
    flags = down(row_flip, col_flip, jnp.zeros((14, LANES), f32)).astype(bf16)
    for dest in range(8):
        x, core = dest // 2, dest % 2
        at = core * (PART_ROWS + SHARED_ROWS)
        for group in range(2):
            lanes = slice((2 * dest + group) * LANES, (2 * dest + group + 1) * LANES)
            row = at + 128 * group
            out_ref[x, row : row + 128, :] = u_ref[:, lanes]
            hi, lo = parts(cot_ref[:, lanes])
            row += TOKEN_ROWS
            out_ref[x, row : row + 128, :] = hi
            out_ref[x, row + 256 : row + 384, :] = lo
        decays = down(*(d_ref[layer, 4 * dest : 4 * dest + 4, :] for layer in range(2)))
        hi, lo = parts(decays)
        out_ref[x, at + 256 : at + 272, :] = down(hi.astype(f32), lo.astype(f32)).astype(bf16)
    for x in range(4):
        for k in range(4):
            at = PART_ROWS + 128 * k
            out_ref[x, at : at + 128, :] = v_ref[k]
        out_ref[x, PART_ROWS + 512 : PART_ROWS + 528, :] = flags


def gather_kernel(
    place_ref, own, other, tok_ref, cot_ref, sh_ref, ends_ref, rows_ref, run_ref, s_ref, a_ref, sems
):
    z, core = place_ref[0], place_ref[2]
    mine = pl.multiple_of(core * (PART_ROWS + SHARED_ROWS), 16)
    part = pl.multiple_of(core * SHARED_ROWS, 16)
    share = pl.multiple_of((1 - core) * PART_ROWS, 16)
    tokens, vectors_in, cotangents = [], [], []
    for x in range(4):
        near, far = 2 * x + core, 2 * x + 1 - core
        tokens += [
            (own.at[x, pl.ds(mine, TOKEN_ROWS)], tok_ref.at[near]),
            (other.at[x, pl.ds(part, TOKEN_ROWS)], tok_ref.at[far]),
        ]
        vectors_in += [
            (own.at[x, pl.ds(PART_ROWS, SHARED_ROWS)], sh_ref.at[near]),
            (other.at[x, pl.ds(share, SHARED_ROWS)], sh_ref.at[far]),
        ]
        cotangents += [
            (own.at[x, pl.ds(mine + TOKEN_ROWS, COT_ROWS)], cot_ref.at[near]),
            (other.at[x, pl.ds(part + TOKEN_ROWS, COT_ROWS)], cot_ref.at[far]),
        ]
    copies = [
        pltpu.make_async_copy(a, b, sems.at[i])
        for i, (a, b) in enumerate(tokens + vectors_in + cotangents)
    ]
    for one in copies:
        one.start()
    c = constants()
    s_ref[...] = jnp.zeros_like(s_ref)
    a_ref[...] = jnp.zeros_like(a_ref)
    for one in copies[:8]:
        one.wait()
    running, layers = decay_rows_of(tok_ref)
    run_ref[...] = running
    for k in range(2):
        rows_ref[k] = layers[k]
    for one in copies[8:16]:
        one.wait()

    def forward(b):
        writes, _ = vectors(sh_ref, b, 0)
        scale = decay_scales(c, rows_ref, b, 0, "left")
        values = [inputs_of(tok_ref, b, g).astype(f32) * scale[g][0] for g in range(2)]
        update(s_ref, [one[1] for one in scale], writes, values)

    def backward(i):
        b = BLOCKS - 1 - i
        _, reads = vectors(sh_ref, b, 1)
        scale = decay_scales(c, rows_ref, b, 1, "grown")
        values = []
        for group in range(2):
            hi, lo = cotangent_of(cot_ref, b, group)
            values.append((hi.astype(f32) + lo.astype(f32)) * scale[group][0])
        update(a_ref, [one[1] for one in scale], reads, values)

    over_blocks(forward, "gather")
    for one in copies[16:]:
        one.wait()
    over_blocks(backward, "gather")
    ends_ref[...] = jnp.where(z == 0, s_ref[...], a_ref[...]).astype(bf16)


def pick_second(source, out_ref, sems):
    load([(source.at[1, x], out_ref.at[x]) for x in range(4)], sems)


def first_forward(place_ref, skip_ref, rows_ref, run_ref, tok_ref, sh_ref, ends_ref, keep_ref, send_ref, state_ref, s_ref):
    z = place_ref[0]
    c = constants()
    s_ref[...] = jnp.where(z == 1, ends_ref[...].astype(f32), 0.0)

    def step(b):
        writes, reads = vectors(sh_ref, b, 0)
        scores = nt(reads, writes)
        turn = mirror(c, sh_ref, b, 0)
        for group, (decay_a, decay_b, grown, left, total) in enumerate(
            decay_block(c, rows_ref, run_ref, b, 0)
        ):
            u = inputs_of(tok_ref, b, group)
            mixed = across(*parts(across(decay_a * scores, decay_b * scores)))
            state = s_ref[group]
            state_both = down(*parts(state))
            state_ref[b, group] = state_both
            u32 = u.astype(f32)
            heads = by_head(c, u)
            y = (
                nn(mixed, down(heads, heads))
                + grown * nn(across(reads, reads), state_both)
                + skip_row(place_ref, skip_ref, group) * u32
            )
            s_ref[group] = update_pair(total, state, writes, u32 * left)
            grid = nn(turn, y.astype(bf16)).astype(bf16)
            for k in range(4):
                near, far = grid[32 * k : 32 * k + 16], grid[32 * k + 16 : 32 * k + 32]
                at = pl.multiple_of(64 * b + 16 * k, 16)
                keep_ref[group, pl.ds(at, 16), :] = jnp.where(z == 0, near, far)
                send_ref[group, pl.ds(at, 16), :] = jnp.where(z == 0, far, near)

    over_blocks(step, "first")


def first_backward(place_ref, skip_ref, rows_ref, run_ref, sh_ref, cot_ref, ends_ref, keep_ref, send_ref, adjoint_ref, a_ref):
    z = place_ref[0]
    c = constants()
    a_ref[...] = jnp.where(z == 0, ends_ref[...].astype(f32), 0.0)

    def step(i):
        b = BLOCKS - 1 - i
        writes, reads = vectors(sh_ref, b, 1)
        scores = nt(reads, writes)
        turn = mirror(c, sh_ref, b, 1)
        for group, (decay_a, decay_b, grown, left, total) in enumerate(
            decay_block(c, rows_ref, run_ref, b, 1)
        ):
            hi, lo = cotangent_of(cot_ref, b, group)
            mixed, mixed_low = parts(down(decay_a * scores, decay_b * scores))
            adjoint = a_ref[group]
            adjoint_both = down(*parts(adjoint))
            adjoint_ref[b, group] = adjoint_both
            dy = hi.astype(f32) + lo.astype(f32)
            hi_heads, lo_heads = by_head(c, hi), by_head(c, lo)
            du = (
                tn(down(mixed, mixed_low, mixed), down(hi_heads, hi_heads, lo_heads))
                + left * nn(across(writes, writes), adjoint_both)
                + skip_row(place_ref, skip_ref, group) * dy
            )
            a_ref[group] = update_pair(total, adjoint, reads, dy * grown)
            grid = nn(turn, du.astype(bf16)).astype(bf16)
            for k in range(2):
                near, far = grid[64 * k : 64 * k + 32], grid[64 * k + 32 : 64 * k + 64]
                at = pl.multiple_of(64 * b + 32 * k, 32)
                keep_ref[group, pl.ds(at, 32), :] = jnp.where(z == 0, near, far)
                send_ref[group, pl.ds(at, 32), :] = jnp.where(z == 0, far, near)

    over_blocks(step, "first")


def regrid_forward(
    place_ref, rows_ref, sh_ref, cot_ref, keep_ref, got_ref, u2_ref, ends_ref, skip_ref, grid_ref, s_ref
):
    z = place_ref[0]
    c = constants()
    grid_ref[z] = keep_ref[...].astype(f32)
    grid_ref[1 - z] = got_ref[...].astype(f32)
    s_ref[...] = jnp.zeros_like(s_ref)
    skip_ref[...] = jnp.zeros_like(skip_ref)

    def step(b):
        writes, _ = vectors(sh_ref, b, 1)
        turn = mirror(c, sh_ref, b, 1)
        scale = decay_scales(c, rows_ref, b, 1, "left")
        values = []
        for group in range(2):
            picked = down(
                *(
                    grid_ref[part, group, pl.ds(2 * b + k, 32, stride=16), :]
                    for k in range(2)
                    for part in range(2)
                )
            )
            u32 = nn(turn, picked.astype(bf16))
            u2_ref[b, group] = u32.astype(bf16)
            values.append(u32 * scale[group][0])
            hi, lo = cotangent_of(cot_ref, b, group)
            dy = hi.astype(f32) + lo.astype(f32)
            skip_ref[group : group + 1, :] += jnp.sum(u32 * dy, axis=0, keepdims=True)
        update(s_ref, [one[1] for one in scale], writes, values)

    over_blocks(step, "regrid")
    ends_ref[...] = s_ref[...].astype(bf16)


def regrid_backward(
    place_ref, rows_ref, tok_ref, sh_ref, keep_ref, got_ref, skip_two_ref, dy1_ref, ends_ref, grid_ref, skip_ref, a_ref
):
    z = place_ref[0]
    c = constants()
    grid_ref[z] = keep_ref[...].astype(f32)
    grid_ref[1 - z] = got_ref[...].astype(f32)
    a_ref[...] = jnp.zeros_like(a_ref)
    skip_ref[0:2, :] = jnp.zeros((2, LANES), f32)
    skip_ref[2:8, :] = skip_two_ref[0:6, :]

    def step(i):
        b = BLOCKS - 1 - i
        _, reads = vectors(sh_ref, b, 0)
        turn = mirror(c, sh_ref, b, 0)
        scale = decay_scales(c, rows_ref, b, 0, "grown")
        values = []
        for group in range(2):
            picked = down(
                *(
                    grid_ref[part, group, pl.ds(4 * b + k, 16, stride=32), :]
                    for k in range(4)
                    for part in range(2)
                )
            )
            dy = nn(turn, picked.astype(bf16))
            dy1_ref[b, group] = dy.astype(bf16)
            values.append(dy * scale[group][0])
            u = inputs_of(tok_ref, b, group).astype(f32)
            skip_ref[group : group + 1, :] += jnp.sum(u * dy, axis=0, keepdims=True)
        update(a_ref, [one[1] for one in scale], reads, values)

    over_blocks(step, "regrid")
    for group in range(2):
        ends_ref[LANES * group : LANES * (group + 1), :] = a_ref[group]
    ends_ref[2 * LANES :, :] = skip_ref[...]


def block_gradients(c, rows_ref, run_ref, sh_ref, b, layer, u_of, dy_of, state_of, adjoint_of):
    writes, reads = vectors(sh_ref, b, layer)
    reads_two, writes_two = down(reads, reads), down(writes, writes)
    scores = nt(reads, writes)
    d_scores, d_writes, d_reads = 0.0, 0.0, 0.0
    decay_rows, kept = [], []
    for group, (decay_a, decay_b, grown, left, total) in enumerate(
        decay_block(c, rows_ref, run_ref, b, layer)
    ):
        u, (dy, dy_low) = u_of(group), dy_of(group)
        u32, dy32 = u.astype(f32), dy.astype(f32)
        dy_heads = by_head(c, dy)
        if dy_low is None:
            pairs = nt(dy_heads, u)
        else:
            pairs = nt(across(dy_heads, by_head(c, dy_low)), across(u, u))
            dy32 = dy32 + dy_low.astype(f32)
        pair_a, pair_b = decay_a * pairs[:BLOCK], decay_b * pairs[BLOCK:]
        d_scores = d_scores + pair_a + pair_b
        u_left, dy_grown = u32 * left, dy32 * grown
        u_hi, u_lo = parts(u_left)
        dy_hi, dy_lo = parts(dy_grown)
        state, adjoint = state_of(group), adjoint_of(group)
        read_state = nn(across(reads, reads), state)
        write_adjoint = nn(across(writes, writes), adjoint)
        state_hi, adjoint_hi = state[:LANES], adjoint[:LANES]
        d_writes = (
            d_writes
            + nt(across(u_hi, u_lo), across(adjoint_hi, adjoint_hi))
        )
        d_reads = (
            d_reads
            + nt(across(dy_hi, dy_lo), across(state_hi, state_hi))
        )
        crossing = across((pair_a * scores).astype(bf16), (pair_b * scores).astype(bf16))
        inner = tn(crossing, c["lower_bf"])
        products = down(
            (dy_grown * read_state).astype(bf16),
            (u_left * write_adjoint).astype(bf16),
            (total * (state_hi.astype(f32) * adjoint_hi.astype(f32))).astype(bf16),
        )
        outer = tn(products, c["sums"])
        for k in range(2):
            decay_rows.append(
                jnp.sum(c["before"] * inner[BLOCK * k : BLOCK * (k + 1)], axis=0, keepdims=True)
                + jnp.sum(outer[HALF * k : HALF * (k + 1)], axis=0, keepdims=True)
            )
        kept.append(
            {
                "total": total,
                "left": left,
                "u_left": down(u_hi, u_lo),
                "dy_grown": down(dy_hi, dy_lo),
                "write_adjoint": write_adjoint,
                "dy_heads": dy_heads,
                "dy": dy32,
                "mixed": lambda a=decay_a, h=decay_b: down(
                    (a * scores).astype(bf16), (h * scores).astype(bf16)
                ),
            }
        )
    low = parts(d_scores)
    d_writes = d_writes + tn(down(*low), reads_two)
    d_reads = d_reads + nn(across(*low), writes_two)
    return d_writes, d_reads, down(*decay_rows), kept, writes_two, reads_two


def put_gradients(out_ref, core, b, at, d_writes, d_reads, rows):
    slot, x = jnp.bitwise_xor(b % 2, core), b // 2
    out_ref[slot, x, at : at + 128, :] = d_writes.astype(bf16)
    out_ref[slot, x, at + 128 : at + 256, :] = d_reads.astype(bf16)
    hi, lo = parts(rows)
    small = down(hi.astype(f32), lo.astype(f32), jnp.zeros((8, LANES), f32))
    out_ref[slot, x, at + 256 : at + 272, :] = small.astype(bf16)


def second_forward(place_ref, rows_ref, run_ref, sh_ref, cot_ref, u2_ref, adjoint_ref, ends_ref, out_ref, s_ref):
    core = place_ref[2]
    c = constants()
    s_ref[...] = ends_ref[...].astype(f32)

    def step(b):
        d_writes, d_reads, rows, kept, writes_two, _ = block_gradients(
            c,
            rows_ref,
            run_ref,
            sh_ref,
            b,
            1,
            lambda g: u2_ref[b, g],
            lambda g: cotangent_of(cot_ref, b, g),
            lambda g: down(*parts(s_ref[g])),
            lambda g: adjoint_ref[b, g],
        )
        put_gradients(out_ref, core, b, 0, d_writes, d_reads, rows)
        for group in range(2):
            k = kept[group]
            s_ref[group] = k["total"] * s_ref[group] + tn(writes_two, k["u_left"])

    over_blocks(step, "second")


def second_backward(
    place_ref, skip_ref, rows_ref, run_ref, tok_ref, sh_ref, dy1_ref, state_ref, ends_ref, own_ref, _second, out_ref, sums_ref, a_ref
):
    core = place_ref[2]
    c = constants()
    for group in range(2):
        arrived = ends_ref[LANES * group : LANES * (group + 1), :]
        a_ref[group] = jnp.where(place_ref[0] == 0, arrived, 0.0)
    total = own_ref[2 * LANES :, :] + ends_ref[2 * LANES :, :]
    for k in range(sums_ref.shape[0]):
        sums_ref[k] = total

    def step(i):
        b = BLOCKS - 1 - i
        d_writes, d_reads, rows, kept, _, reads_two = block_gradients(
            c,
            rows_ref,
            run_ref,
            sh_ref,
            b,
            0,
            lambda g: inputs_of(tok_ref, b, g),
            lambda g: (dy1_ref[b, g], None),
            lambda g: state_ref[b, g],
            lambda g: down(*parts(a_ref[g])),
        )
        put_gradients(out_ref, core, b, 256, d_writes, d_reads, rows)
        slot = jnp.bitwise_xor(b % 2, core)
        for group in range(2):
            k = kept[group]
            du = (
                tn(k["mixed"](), k["dy_heads"])
                + k["left"] * k["write_adjoint"]
                + skip_row(place_ref, skip_ref, group) * k["dy"]
            )
            out_ref[slot, b // 2, 128 * group : 128 * group + 128, :] = du.astype(bf16)
            a_ref[group] = k["total"] * a_ref[group] + tn(reads_two, k["dy_grown"])

    over_blocks(step, "second")


def pair_kernel(own_ref, other_ref, own_two_ref, other_two_ref, skip_ref, skip_other_ref, out_ref):
    skips = []
    for ref in (skip_ref, skip_other_ref):
        total = ref[0, 0:4, :]
        for k in range(1, ref.shape[0]):
            total = total + ref[k, 0:4, :]
        hi = total.astype(bf16).astype(f32)
        mid, low = parts(total - hi)
        skips.append(down(hi, mid.astype(f32), low.astype(f32), jnp.zeros((4, LANES), f32)))
    skips = down(*skips).astype(bf16)
    for x in range(4):
        out_ref[x, 0:256, :] = own_ref[0, x, 0:256, :]
        out_ref[x, 256:512, :] = other_ref[x, 0:256, :]
        out_ref[x, 512:768, :] = (
            own_ref[0, x, 256:512, :].astype(f32) + other_ref[x, 256:512, :].astype(f32)
        ).astype(bf16)
        out_ref[x, 768:784, :] = own_ref[0, x, 512:528, :]
        out_ref[x, 784:800, :] = other_ref[x, 512:528, :]
        out_ref[x, 800:832, :] = skips
        out_ref[x, 832:1088, :] = (
            own_two_ref[0, x, 0:256, :].astype(f32) + other_two_ref[x, 0:256, :].astype(f32)
        ).astype(bf16)
        out_ref[x, 1088:1104, :] = own_two_ref[0, x, 256:272, :]
        out_ref[x, 1104:1120, :] = other_two_ref[x, 256:272, :]


def last_kernel(place_ref, back_ref, grad_ref, w1, r1, w2, r2, decay1_ref, decay2_ref, skip1_ref, skip2_ref):
    core = place_ref[2]

    def chosen(ref, x, at, size, owner):
        near, far = ref[x, at : at + size, :], ref[x, at + size : at + 2 * size, :]
        return jnp.where(core == owner, near, far)

    lanes = []
    for x in range(4):
        for owner in range(2):
            both = chosen(back_ref, x, 0, 256, owner)
            for group in range(2):
                at = ((2 * x + owner) * 2 + group) * LANES
                grad_ref[:, at : at + LANES] = both[128 * group : 128 * group + 128]
            at = (2 * x + owner) * 4
            small = chosen(back_ref, x, 768, 16, owner).astype(f32)
            decay1_ref[at : at + 4, :] = small[0:4] + small[4:8]
            small = chosen(back_ref, x, 1088, 16, owner).astype(f32)
            decay2_ref[at : at + 4, :] = small[0:4] + small[4:8]
            small = chosen(back_ref, x, 800, 16, owner).astype(f32)
            lanes.append(small[0:4] + small[4:8] + small[8:12])
    lanes = down(*lanes)
    row, head = (lax.broadcasted_iota(jnp.int32, (32, 32), k) for k in range(2))
    lane, side = (lax.broadcasted_iota(jnp.int32, (LANES, 32), k) for k in range(2))
    folded = lax.dot_general(
        lanes,
        one_where(lane // HALF == side % 2),
        (((1,), (0,)), ((), ())),
        precision=lax.Precision.HIGHEST,
        preferred_element_type=f32,
    )
    owner = (row // 4 == head // 4) & (row % 2 == head // 2 % 2)
    for layer, ref in enumerate((skip1_ref, skip2_ref)):
        kept = jnp.where(owner & (row // 2 % 2 == layer), folded, 0.0)
        ref[...] = jnp.sum(kept, axis=0, keepdims=True) * SKIP_SCALE
    for ref, at in ((w1, 512), (r1, 640), (w2, 832), (r2, 960)):
        total = back_ref[0, at : at + 128, :].astype(f32)
        for x in range(1, 4):
            total = total + back_ref[x, at : at + 128, :].astype(f32)
        ref[...] = total.astype(bf16)


def call(kernel, outs, scratch, *args, scalars=1, anywhere=(), copies=0, us=5, mib=12):
    shapes = [jax.ShapeDtypeStruct(s, d) for s, d in outs]
    many = len(shapes) > 1
    in_specs = [
        pl.BlockSpec(
            memory_space=pltpu.SMEM if i < scalars else pl.ANY if i in anywhere else pltpu.VMEM
        )
        for i in range(len(args))
    ]
    out_specs = [pl.BlockSpec(memory_space=pltpu.VMEM)] * len(shapes)
    scratch = [pltpu.VMEM(s, d) for s, d in scratch]
    if copies:
        scratch.append(pltpu.SemaphoreType.DMA((copies,)))
    return pl.pallas_call(
        kernel,
        out_shape=shapes if many else shapes[0],
        in_specs=in_specs,
        out_specs=out_specs if many else out_specs[0],
        scratch_shapes=scratch,
        cost_estimate=pl.CostEstimate(flops=us * 10**9, bytes_accessed=10**6, transcendentals=0),
        compiler_params=pltpu.CompilerParams(vmem_limit_bytes=mib * 2**20),
        name=kernel.__name__,
    )(*args)


def pick_slot(values):
    out = (values.shape[1:], bf16)
    return call(pick_second, [out], [], values, scalars=0, anywhere=(0,), copies=4, us=1)


def swap(values, axis):
    return lax.ppermute(values, axis, [(0, 1), (1, 0)])


def over_x(values):
    return lax.all_to_all(values, "x", split_axis=0, concat_axis=0, tiled=True)


def on_device(
    layer_input,
    writes_first,
    reads_first,
    decay_first,
    skip_first,
    writes_second,
    reads_second,
    decay_second,
    skip_second,
    order_first,
    order_second,
    cotangent,
):
    length, features = layer_input.shape[1:]
    head_count = skip_first.shape[0]
    head_size = features // head_count
    z, x, core = (lax.axis_index(a) for a in ("z", "x", "core"))
    place = jnp.stack([z, x, core]).astype(jnp.int32)

    own = over_x(
        call(
            pack_kernel,
            [((4, SEND_ROWS, LANES), bf16)],
            [
                ((length, features), bf16),
                ((2, head_count, length), f32),
                ((4, length, LANES), bf16),
                ((2, 1, length), jnp.int32),
                ((length, features), f32),
            ],
            layer_input[0],
            decay_first[0],
            decay_second[0],
            writes_first[0],
            reads_first[0],
            writes_second[0],
            reads_second[0],
            order_first.reshape(1, length),
            order_second.reshape(1, length),
            cotangent[0],
            scalars=0,
            anywhere=range(10),
            mib=60,
            copies=10,
            us=2,
        )
    )
    theirs = lax.dynamic_slice_in_dim(own, (1 - core) * PART_ROWS, PART_ROWS + SHARED_ROWS, axis=1)
    other = swap(theirs, "core")

    carry = ((2, LANES, LANES), f32)
    sent = ((2, LANES, LANES), bf16)
    saved = ((BLOCKS, 2, 2 * LANES, LANES), bf16)
    half_grid = ((2, 512, LANES), bf16)
    block = ((BLOCKS, 2, BLOCK, LANES), bf16)
    grids = ((2, 2, 512, LANES), f32)
    few = ((8, LANES), f32)

    tok, cot, sh, end, rows, run = call(
        gather_kernel,
        [
            ((BLOCKS, TOKEN_ROWS, LANES), bf16),
            ((BLOCKS, COT_ROWS, LANES), bf16),
            ((BLOCKS, SHARED_ROWS, LANES), bf16),
            sent,
            ((2, BLOCKS, 32, LANES), bf16),
            ((BLOCKS, 8, LANES), f32),
        ],
        [carry, carry],
        place,
        own,
        other,
        anywhere=(1, 2),
        copies=24,
    )
    end = swap(end, "z")
    keep, send, states = call(
        first_forward,
        [half_grid, half_grid, saved],
        [carry],
        place,
        skip_first,
        rows,
        run,
        tok,
        sh,
        end,
        scalars=2,
    )
    got = swap(send, "z")
    keep_back, send_back, adjoints = call(
        first_backward,
        [half_grid, half_grid, saved],
        [carry],
        place,
        skip_second,
        rows,
        run,
        sh,
        cot,
        end,
        scalars=2,
    )
    got_back = swap(send_back, "z")
    u2, end, skip_two = call(
        regrid_forward, [block, sent, few], [grids, carry], place, rows, sh, cot, keep, got
    )
    end = lax.ppermute(end, "z", [(0, 1)])
    dy1, end_own = call(
        regrid_backward,
        [block, ((2 * LANES + 8, LANES), f32)],
        [grids, few, carry],
        place,
        rows,
        tok,
        sh,
        keep_back,
        got_back,
        skip_two,
    )
    end_back = swap(end_own, "z")

    out_two = call(
        second_forward,
        [((2, 4, 272, LANES), bf16)],
        [carry],
        place,
        rows,
        run,
        sh,
        cot,
        u2,
        adjoints,
        end,
        us=8,
    )
    clips = lax.axis_size("dp")
    out, skip_sums = call(
        second_backward,
        [((2, 4, 528, LANES), bf16), ((clips, 8, LANES), f32)],
        [carry],
        place,
        skip_first,
        rows,
        run,
        tok,
        sh,
        dy1,
        states,
        end_back,
        end_own,
        out_two,
        scalars=2,
        anywhere=(10,),
        us=8,
    )
    skip_sums = lax.all_to_all(skip_sums, "dp", split_axis=0, concat_axis=0, tiled=True)
    back = over_x(
        call(
            pair_kernel,
            [((4, 1120, LANES), bf16)],
            [],
            out,
            swap(pick_slot(out), "core"),
            out_two,
            swap(pick_slot(out_two), "core"),
            skip_sums,
            swap(skip_sums, "core"),
            scalars=0,
            us=1,
        )
    )
    vector = ((length, LANES), bf16)
    decay = ((head_count, length), f32)
    skip = ((1, head_count), f32)
    grad_input, w1, r1, w2, r2, decay1, decay2, skip1, skip2 = call(
        last_kernel,
        [((length, features), bf16), vector, vector, vector, vector, decay, decay, skip, skip],
        [],
        place,
        back,
        us=1,
    )
    return (
        grad_input[None],
        w1[None],
        r1[None],
        decay1[None],
        skip1.reshape(head_count),
        w2[None],
        r2[None],
        decay2[None],
        skip2.reshape(head_count),
    )


def solution(mesh):
    finer = Mesh(mesh.devices.reshape(-1, 2, 4, 2), ("dp", "z", "x", "core"))
    seq = ("z", "x", "core")
    by_token, by_decay = P("dp", seq, None), P("dp", None, seq)
    return jax.shard_map(
        on_device,
        mesh=finer,
        in_specs=(
            by_token,
            by_token,
            by_token,
            by_decay,
            P(),
            by_token,
            by_token,
            by_decay,
            P(),
            P(seq),
            P(seq),
            by_token,
        ),
        out_specs=(
            by_token,
            by_token,
            by_token,
            by_decay,
            P(),
            by_token,
            by_token,
            by_decay,
            P(),
        ),
        check_vma=False,
    )
```
